256 devices in a mesh: gx: 32 (over y, x, core), gy: 8 (over z).
Axes of the slice: x: 4, y: 4, z: 8, core: 2. Of those that a mesh axis runs over, the one named last changes fastest.
Arguments:
- corpus: bfloat16 [262144, 1024], P(('gx', 'gy')), may hold values from -6 to 6
- rotation: bfloat16 [1024, 1024], replicated, may hold values from -0.1875 to 0.1875
- code_table: int32 [262144, 64], P(('gx', 'gy')), may hold values from 0 to 255
- codebooks: bfloat16 [64, 256, 16], replicated, may hold values from -6 to 6
Outputs:
- new_rotation: float32 [1024, 1024], P('gx')
- distortion: float32 [262144], P(('gx', 'gy'))
The draws below stay inside these ranges and needn't reach their ends.
All inputs are finite; a program needn't handle non-finite values.
Results may differ from the reference program's by a relative error of at most 0.0003.
Values sent between devices are 32-bit elements; how exact they have to be, the bound alone decides.
No kernel may reach another device: no remote copies, remote signals or barrier semaphores. Data moves between devices by JAX's collectives and lax.ppermute only.
A program may use at most 64 MiB of HBM per device.

```python
import math
import jax
import jax.numpy as jnp
from jax import lax

D = 1024
SUB = 64
KCODE = 256
SUBW = 16
ROWS_DEV = 1024
ITERS = 4
ROWS_ALL = 262144
DEVICES = 256


def place_ends(values, stream_key, least, top_value):
    longest = values.shape.index(max(values.shape))
    spots = []
    for shift in (0, 1):
        where = [jax.random.randint(jax.random.fold_in(stream_key, axis), (), 0, length) for axis, length in enumerate(values.shape)]
        where[longest] = (where[longest] + shift) % values.shape[longest]
        spots.append(tuple(where))
    return values.at[spots[0]].set(least).at[spots[1]].set(top_value)


def block_levels(stream_key, extent, split, smallest, top_value):
    factor_of = 1.0
    for position, shards_of in split:
        heights = jax.random.uniform(jax.random.fold_in(jax.random.fold_in(stream_key, 6), position), (shards_of,), jnp.float32, smallest / len(split), top_value / len(split))
        factor_of = factor_of * jnp.repeat(jnp.exp(heights), extent[position] // shards_of).reshape((-1,) + (1,) * (len(extent) - 1 - position))
    return factor_of


def bell_draw(rng, shape, scale, reach, pieces=(), kind=jnp.bfloat16):
    level = block_levels(rng, shape, pieces, -0.22, 0.18) if pieces else 1.0
    values = jax.random.normal(rng, shape, jnp.float32) * scale * level
    return jnp.minimum(jnp.maximum(values, -reach), reach).astype(kind)


def setup_inputs(seed: int = 0) -> dict:
    key_of = jax.random.split(jax.random.key(seed), 5)
    corpus = bell_draw(key_of[0], (ROWS_ALL, D), 1.0, 6.0, ((0, 256),))
    rotation = bell_draw(key_of[1], (D, D), D ** -0.5, 0.1875)
    code_table = place_ends(jax.random.randint(key_of[2], (ROWS_ALL, SUB), 0, KCODE), jax.random.fold_in(key_of[2], 1), 0, KCODE - 1).astype(jnp.int32)
    codebooks = bell_draw(key_of[3], (SUB, KCODE, SUBW), 1.0, 6.0)
    return dict(corpus=corpus, rotation=rotation, code_table=code_table, codebooks=codebooks)


def rebuild_block(block_codes, codebooks):
    index_sub = jnp.arange(codebooks.shape[0], dtype=jnp.int32)
    picked = codebooks[index_sub[None, :], block_codes]
    return picked.reshape(block_codes.shape[0], -1)

def reference(corpus, rotation, code_table, codebooks):
    row_scale = 1.0 / math.sqrt(ROWS_ALL)
    corpus_blocks = corpus.reshape(DEVICES, ROWS_DEV, D)
    code_blocks = code_table.reshape(DEVICES, ROWS_DEV, SUB)

    def one_block(cross_sum, inputs_pair):
        block_rows, block_codes = inputs_pair
        rebuilt = rebuild_block(block_codes, codebooks)
        rotated = jnp.dot(block_rows, rotation, preferred_element_type=jnp.float32)
        mismatch = rotated - rebuilt.astype(jnp.float32)
        distortion_block = lax.optimization_barrier(jnp.sum(mismatch * mismatch, axis=1))
        term = lax.dot_general(block_rows, rebuilt, (((0,), (0,)), ((), ())), preferred_element_type=jnp.float32)
        return (cross_sum + term * row_scale, distortion_block)
    cross, distortion_all = lax.scan(one_block, jnp.zeros((D, D), jnp.float32), (corpus_blocks, code_blocks))
    products = jnp.dot(cross, cross.T, precision=lax.Precision.HIGHEST)
    square_sum = jnp.sum(products * products)
    current = cross * (square_sum + 1e-06) ** (-0.25)
    for iteration in range(ITERS):
        gram_rows = jnp.dot(current, current.T, precision=lax.Precision.HIGHEST)
        current = 1.5 * current - 0.5 * jnp.dot(gram_rows, current, precision=lax.Precision.HIGHEST)
    return (current * math.sqrt(D), distortion_all.reshape(ROWS_ALL))
```

```python
import math, functools
import jax, jax.numpy as jnp
from jax import lax
from jax.sharding import PartitionSpec as P
from jax.experimental import pallas as pl
from jax.experimental.pallas import tpu as pltpu

BF, F32 = jnp.bfloat16, jnp.float32
MIB = 1 << 20

def split(x):
    hi = x.astype(BF)
    return hi, (x - hi.astype(F32)).astype(BF)

def nt(a, b):
    return lax.dot_general(a, b, (((1,), (1,)), ((), ())), preferred_element_type=F32)

def nn(a, b):
    return lax.dot_general(a, b, (((1,), (0,)), ((), ())), preferred_element_type=F32)

def cross_kernel(scale, half_ref, codes_ref, books_ref, corpus_ref, out_ref, reb_ref):
    subs, width, words = books_ref.shape
    rows = codes_ref.shape[1]
    word = lax.broadcasted_iota(jnp.int16, (words, rows), 0)
    codes = codes_ref[...].astype(jnp.int16)
    one, zero = jnp.ones((), BF), jnp.zeros((), BF)
    for s in range(subs):
        hot = jnp.where(word == codes[s:s + 1, :], one, zero)
        reb_ref[s * width:(s + 1) * width, :] = nn(books_ref[s], hot).astype(BF)
    out_ref[...] = nn(reb_ref[...], corpus_ref[...]) * scale

def cross_half(half, codes_t, books_t, corpus, scale, chunk=16):
    subs, width, words = books_t.shape
    rows, d = corpus.shape
    steps = subs // 2 // chunk
    return pl.pallas_call(
        functools.partial(cross_kernel, scale),
        grid_spec=pltpu.PrefetchScalarGridSpec(
            num_scalar_prefetch=1, grid=(steps,),
            in_specs=[pl.BlockSpec((chunk, rows), lambda i, h: (h[0] * steps + i, 0)),
                      pl.BlockSpec((chunk, width, words), lambda i, h: (h[0] * steps + i, 0, 0)),
                      pl.BlockSpec((rows, d), lambda i, h: (0, 0))],
            out_specs=[pl.BlockSpec((chunk * width, d), lambda i, h: (i, 0)),
                       pl.BlockSpec((chunk * width, rows), lambda i, h: (i, 0))]),
        out_shape=[jax.ShapeDtypeStruct((subs // 2 * width, d), F32),
                   jax.ShapeDtypeStruct((subs // 2 * width, rows), BF)],
        compiler_params=pltpu.CompilerParams(vmem_limit_bytes=40 * MIB),
        name="cross_half",
    )(half, codes_t, books_t, corpus)

def dist_kernel(half_ref, rot_ref, corpus_ref, reb_ref, out_ref):
    rotated = lax.dot_general(rot_ref[...], corpus_ref[...], (((0,), (1,)), ((), ())), preferred_element_type=F32)
    gap = rotated - reb_ref[...].astype(F32)
    out_ref[...] = jnp.sum(gap * gap, axis=0, keepdims=True)

def dist_half(half, rotation, corpus, reb):
    d = rotation.shape[0]
    rows = corpus.shape[0]
    cols = reb.shape[0]
    return pl.pallas_call(
        dist_kernel,
        grid_spec=pltpu.PrefetchScalarGridSpec(
            num_scalar_prefetch=1, grid=(1,),
            in_specs=[pl.BlockSpec((d, cols), lambda i, h: (0, h[0])),
                      pl.BlockSpec((rows, d), lambda i, h: (0, 0)),
                      pl.BlockSpec((cols, rows), lambda i, h: (0, 0))],
            out_specs=pl.BlockSpec((1, rows), lambda i, h: (0, 0))),
        out_shape=jax.ShapeDtypeStruct((1, rows), F32),
        compiler_params=pltpu.CompilerParams(vmem_limit_bytes=40 * MIB),
        name="dist_half",
    )(half, rotation, corpus, reb)

def polar_kernel(place_ref, own_ref, oth_ref, out_ref, yh, yl, gh, gl, th, tl, gf, tf):
    n = yh.shape[0]
    half = n // 2
    blk = 256
    nb = n // blk
    h, l = split(own_ref[...])
    yh[:half, :] = h
    yl[:half, :] = l
    h, l = split(oth_ref[...])
    yh[half:, :] = h
    yl[half:, :] = l

    def spans(i):
        return slice(i * blk, (i + 1) * blk), slice(i * blk, n)

    def put(dh, dl, i, val):
        r, c = spans(i)
        h, l = split(val)
        dh[r, c] = h
        dl[r, c] = l
        for j in range(i + 1, nb):
            t = val[:, (j - i) * blk:(j - i + 1) * blk].T
            h, l = split(t)
            dh[j * blk:(j + 1) * blk, r] = h
            dl[j * blk:(j + 1) * blk, r] = l

    def sym(lh, ll, rh, rl, i):
        r, c = spans(i)
        a, b = lh[r, :], ll[r, :]
        return nn(a, rh[:, c]) + (nn(a, rl[:, c]) + nn(b, rh[:, c]))

    total = jnp.zeros((), F32)
    for i in range(nb):
        r, c = spans(i)
        a, b = yh[r, :], yl[r, :]
        g = nt(a, yh[c, :]) + (nt(a, yl[c, :]) + nt(b, yh[c, :]))
        gf[r, c] = g
        put(gh, gl, i, g)
        sq = g * g
        total = total + 2.0 * jnp.sum(sq) - jnp.sum(sq[:, :blk])
    base = jnp.full((8, 128), total + 1e-06, F32)
    root = lax.rsqrt(base)
    f2 = jnp.max(root)
    f1 = jnp.max(jnp.sqrt(root))

    def thin(ah, al, cur):
        h, l = split(cur)
        w = jnp.concatenate([h, l], axis=1)
        p = nn(ah[...], w)
        k = cur.shape[1]
        return p[:, :k] + (p[:, k:] + nn(al[...], h))

    col = pl.multiple_of(place_ref[1] * 128, 128)
    cur = jnp.concatenate([own_ref[:, pl.ds(col, 128)], oth_ref[:, pl.ds(col, 128)]], axis=0) * f1
    cur = 1.5 * cur - (0.5 * f2) * thin(gh, gl, cur)

    def advance(sh, sl, sf, scale, dh, dl, df, mh, ml, mf):
        for i in range(nb):
            r, c = spans(i)
            m = (1.5 * scale) * sf[r, c] - (0.5 * scale * scale) * sym(sh, sl, sh, sl, i)
            mf[r, c] = m
            put(mh, ml, i, m)
        for i in range(nb):
            r, c = spans(i)
            d = 1.5 * mf[r, c] - (0.5 * scale) * sym(mh, ml, sh, sl, i)
            df[r, c] = d
            put(dh, dl, i, d)

    advance(gh, gl, gf, f2, yh, yl, gf, th, tl, tf)
    cur = 1.5 * cur - 0.5 * thin(yh, yl, cur)
    advance(yh, yl, gf, 1.0, gh, gl, gf, th, tl, tf)
    cur = 1.5 * cur - 0.5 * thin(gh, gl, cur)
    u = thin(gh, gl, cur)
    u = 1.5 * u - 0.5 * thin(gh, gl, u)
    u = 1.5 * u - 0.5 * thin(gh, gl, u)
    cur = (1.5 * cur - 0.5 * u) * math.sqrt(n)
    low = place_ref[0]
    flip = cur.T
    tf[:128, :] = flip
    off = pl.multiple_of(place_ref[2] * 32, 32)
    a = tf[pl.ds(off, 32), :half]
    b = tf[pl.ds(off, 32), half:]
    out_ref[:, :half] = jnp.where(low == 0, a, b)
    out_ref[:, half:] = jnp.where(low == 0, b, a)

def polar(place, own, oth):
    half, n = own.shape
    bf = pltpu.VMEM((n, n), BF)
    return pl.pallas_call(
        polar_kernel,
        in_specs=[pl.BlockSpec(memory_space=pltpu.SMEM)] + [pl.BlockSpec(memory_space=pltpu.VMEM)] * 2,
        out_specs=pl.BlockSpec(memory_space=pltpu.VMEM),
        out_shape=jax.ShapeDtypeStruct((32, n), F32),
        scratch_shapes=[bf, bf, bf, bf, bf, bf, pltpu.VMEM((n, n), F32), pltpu.VMEM((n, n), F32)],
        compiler_params=pltpu.CompilerParams(vmem_limit_bytes=48 * MIB),
        name="polar",
    )(place, own, oth)


AXES = ("gx", "gy")
CORES, SIDE, DEPTH = 2, 4, 8


def place_of(y, x, c, z):
    return ((y * SIDE + x) * CORES + c) * DEPTH + z


def ring_pairs(n, odd):
    pairs = [((i + odd) % n, (i + 1 + odd) % n) for i in range(0, n, 2)]
    return [p if k % 2 == 0 else p[::-1] for k, p in enumerate(pairs)]


def cube_groups():
    return [
        [place_of(y, x, c, z) for y in py for x in px for z in pz]
        for c in range(CORES)
        for py in ring_pairs(SIDE, c)
        for px in ring_pairs(SIDE, c)
        for pz in ring_pairs(DEPTH, c)
    ]


def swap(fn):
    return [
        (place_of(y, x, c, z), place_of(*fn(y, x, c, z)))
        for y in range(SIDE) for x in range(SIDE) for c in range(CORES) for z in range(DEPTH)
    ]


def mate(n, odd):
    table = {}
    for i in range(0, n, 2):
        a, b = (i + odd) % n, (i + 1 + odd) % n
        table[a], table[b] = b, a
    return table


def far(c):
    table = {}
    for a, b in ((0, 3), (4, 7), (2, 5), (6, 1)):
        a, b = (a + c) % DEPTH, (b + c) % DEPTH
        table[a], table[b] = b, a
    return table


SWAP_CORE = swap(lambda y, x, c, z: (y, x, 1 - c, z))
SWAP_X = swap(lambda y, x, c, z: (y, mate(SIDE, 1 - c)[x], c, z))
SWAP_Y = swap(lambda y, x, c, z: (mate(SIDE, 1 - c)[y], x, c, z))
SWAP_Z = swap(lambda y, x, c, z: (y, x, c, mate(DEPTH, 1 - c)[z]))
SWAP_FAR = swap(lambda y, x, c, z: (y, x, c, far(c)[z]))


def send(value, pairs):
    return lax.ppermute(value, AXES, pairs)


def reduce_half(value, bit, pairs):
    half = value.shape[0] // 2
    away = lax.dynamic_slice_in_dim(value, (1 - bit) * half, half, 0)
    keep = lax.dynamic_slice_in_dim(value, bit * half, half, 0)
    return keep + send(away, pairs)


def gather_half(value, bit, pairs):
    other = send(value, pairs)
    return jnp.where(bit == 0, jnp.concatenate([value, other]), jnp.concatenate([other, value]))


def body(corpus, rotation, code_table, codebooks):
    rows, d = corpus.shape
    gx = lax.axis_index("gx")
    core = gx % CORES
    bit_x = gx // CORES % 2
    bit_y = gx // CORES // SIDE % 2
    codes_t = code_table.T
    books_t = codebooks.transpose(0, 2, 1)
    scale = 1.0 / math.sqrt(rows * lax.axis_size("gx") * lax.axis_size("gy"))

    far_half, near_half = (1 - core).reshape(1), core.reshape(1)
    far_term, far_words = cross_half(far_half, codes_t, books_t, corpus, scale)
    arrived = send(far_term, SWAP_CORE)
    near_term, near_words = cross_half(near_half, codes_t, books_t, corpus, scale)
    gaps = dist_half(far_half, rotation, corpus, far_words) + dist_half(near_half, rotation, corpus, near_words)

    groups = cube_groups()
    members = len(groups[0])
    summed = (near_term + arrived).reshape(members, -1, d)
    pieces = lax.all_to_all(summed, AXES, 0, 0, axis_index_groups=groups)
    piece = jnp.sum(pieces, axis=0)

    quarter = reduce_half(piece, bit_x, SWAP_X)
    part = reduce_half(quarter, bit_y, SWAP_Y)
    part = part + send(part, SWAP_Z)
    part = part + send(part, SWAP_FAR)
    quarter = gather_half(part, bit_y, SWAP_Y)
    piece = gather_half(quarter, bit_x, SWAP_X)

    own = lax.all_to_all(jnp.broadcast_to(piece[None], (members,) + piece.shape), AXES, 0, 0, axis_index_groups=groups)
    own = own.reshape(-1, d)
    other = send(own, SWAP_CORE)
    place = jnp.stack([core, gx // 4, gx % 4])
    return polar(place, own, other), gaps.reshape(rows)


def solution(mesh):
    return jax.shard_map(
        body,
        mesh=mesh,
        in_specs=(P(("gx", "gy"), None), P(), P(("gx", "gy"), None), P()),
        out_specs=(P("gx", None), P(("gx", "gy"))),
        check_vma=False,
    )
```

```python
import math, functools
import numpy as np
import jax, jax.numpy as jnp
from jax import lax
from jax.sharding import PartitionSpec as P
from jax.experimental import pallas as pl
from jax.experimental.pallas import tpu as pltpu

BF, F32 = jnp.bfloat16, jnp.float32
MIB = 1 << 20
BLK = 256
ITERS = 4
CHUNK = 16

def split(x):
    hi = x.astype(BF)
    return hi, (x - hi.astype(F32)).astype(BF)

def nt(a, b):
    return lax.dot_general(a, b, (((1,), (1,)), ((), ())), preferred_element_type=F32)

def nn(a, b):
    return lax.dot_general(a, b, (((1,), (0,)), ((), ())), preferred_element_type=F32)

def rebuild(codes, books, words, row, word_at):
    subs = words.shape[0] // books.shape[1]
    width = books.shape[1]
    word = lax.broadcasted_iota(jnp.int16, (books.shape[2], codes.shape[1]), 0)
    one, zero = jnp.ones((), BF), jnp.zeros((), BF)
    for block in range(subs // CHUNK):
        picks = codes[pl.ds(row + block * CHUNK, CHUNK), :].astype(jnp.int16)
        for k in range(CHUNK):
            s = block * CHUNK + k
            hot = jnp.where(word == picks[k:k + 1, :], one, zero)
            words[s * width:(s + 1) * width, :] = nn(books[word_at + s], hot).astype(BF)


def first_kernel(scale, half_ref, codes_hbm, books_hbm, corpus_hbm, out, words_hbm, codes, books, corpus, words, sems):
    subs = books.shape[0]
    first = pl.multiple_of(half_ref[0] * subs, subs)
    loads = [
        pltpu.make_async_copy(codes_hbm.at[pl.ds(first, subs)], codes, sems.at[0]),
        pltpu.make_async_copy(books_hbm.at[pl.ds(first, subs)], books, sems.at[1]),
        pltpu.make_async_copy(corpus_hbm, corpus, sems.at[2]),
    ]
    for load in loads:
        load.start()
    loads[0].wait()
    loads[1].wait()
    rebuild(codes, books, words, 0, 0)
    stores = [pltpu.make_async_copy(words, words_hbm, sems.at[3])]
    stores[0].start()
    loads[2].wait()
    for k in range(corpus.shape[1] // BLK):
        c = slice(k * BLK, (k + 1) * BLK)
        out[:, c] = nn(words[...], corpus[:, c]) * scale
    stores[0].wait()


def cross_first(half, codes_t, books_t, corpus, scale):
    subs, width, size = books_t.shape
    rows, d = corpus.shape
    part = subs // 2
    return pl.pallas_call(
        functools.partial(first_kernel, scale),
        in_specs=[pl.BlockSpec(memory_space=pltpu.SMEM)] + [pl.BlockSpec(memory_space=pl.ANY)] * 3,
        out_specs=[pl.BlockSpec(memory_space=pltpu.VMEM), pl.BlockSpec(memory_space=pltpu.HBM)],
        out_shape=[jax.ShapeDtypeStruct((part * width, d), F32), pltpu.HBM((part * width, rows), BF)],
        scratch_shapes=[
            pltpu.VMEM((part, rows), jnp.int32),
            pltpu.VMEM((part, width, size), BF),
            pltpu.VMEM((rows, d), BF),
            pltpu.VMEM((part * width, rows), BF),
            pltpu.SemaphoreType.DMA((4,)),
        ],
        compiler_params=pltpu.CompilerParams(vmem_limit_bytes=24 * MIB),
        name="cross_first",
    )(half, codes_t, books_t, corpus)


def dist_kernel(half_ref, rot_hbm, corpus_hbm, words_hbm, out_ref, rot, corpus, words, sems):
    cols = words.shape[0]
    first = pl.multiple_of(half_ref[0] * cols, cols)
    loads = [
        pltpu.make_async_copy(corpus_hbm, corpus, sems.at[0]),
        pltpu.make_async_copy(rot_hbm.at[:, pl.ds(first, cols)], rot, sems.at[1]),
        pltpu.make_async_copy(words_hbm, words, sems.at[2]),
    ]
    for load in loads:
        load.start()
    for load in loads:
        load.wait()
    rotated = lax.dot_general(rot[...], corpus[...], (((0,), (1,)), ((), ())), preferred_element_type=F32)
    gap = rotated - words[...].astype(F32)
    out_ref[...] = jnp.sum(gap * gap, axis=0, keepdims=True)


def distortion(half, rotation, corpus, words):
    rows, d = corpus.shape
    cols = words.shape[0]
    return pl.pallas_call(
        dist_kernel,
        in_specs=[pl.BlockSpec(memory_space=pltpu.SMEM)] + [pl.BlockSpec(memory_space=pl.ANY)] * 3,
        out_specs=pl.BlockSpec(memory_space=pltpu.VMEM),
        out_shape=jax.ShapeDtypeStruct((1, rows), F32),
        scratch_shapes=[
            pltpu.VMEM((d, cols), BF),
            pltpu.VMEM((rows, d), BF),
            pltpu.VMEM((cols, rows), BF),
            pltpu.SemaphoreType.DMA((3,)),
        ],
        compiler_params=pltpu.CompilerParams(vmem_limit_bytes=24 * MIB),
        name="distortion",
    )(half, rotation, corpus, words)


def polar_polynomial(steps):
    poly = np.polynomial.polynomial
    e, out = np.array([0.0, 1.0]), np.array([1.0])
    for _ in range(steps):
        out = poly.polymul(out, poly.polyadd([1.0], 0.5 * e))
        sq = poly.polymul(e, e)
        e = poly.polyadd(0.75 * sq, 0.25 * poly.polymul(sq, e))
    return [float(v) for v in out]


def put(hi, lo, i, first, val):
    r = slice(i * BLK, (i + 1) * BLK)
    last = first + val.shape[1]
    hi[r, first:last], lo[r, first:last] = split(val)
    begin = max(first, (i + 1) * BLK)
    if begin < last:
        hi[begin:last, r], lo[begin:last, r] = split(val[:, begin - first:].T)


def gram(hi, lo, i, first, last):
    r, c = slice(i * BLK, (i + 1) * BLK), slice(first, last)
    return nt(hi[r, :], hi[c, :]) + (nt(hi[r, :], lo[c, :]) + nt(lo[r, :], hi[c, :]))


def square(hi, lo, i):
    r, c = slice(i * BLK, (i + 1) * BLK), slice(i * BLK, hi.shape[0])
    return nn(hi[r, :], hi[:, c]) + (nn(hi[r, :], lo[:, c]) + nn(lo[r, :], hi[:, c]))


def thin(u, hi, lo):
    h, l = split(u)
    m = u.shape[0]
    p = nn(jnp.concatenate([h, l], axis=0), hi[...])
    return p[:m] + (p[m:] + nn(h, lo[...]))


def polar_kernel(coef, place_ref, own_ref, oth_hbm, out_ref, oth, yh, yl, gh, gl, bh, bl, gf, bf, turned, sem):
    n = yh.shape[0]
    half = n // 2
    blocks = n // BLK
    rows = out_ref.shape[0]
    load = pltpu.make_async_copy(oth_hbm, oth, sem)
    load.start()
    col = pl.multiple_of(place_ref[1] * 128, 128)
    yh[:half, :], yl[:half, :] = split(own_ref[...])
    turned[:, :half] = own_ref[:, pl.ds(col, 128)].T
    total = jnp.zeros((), F32)
    for i in range(half // BLK):
        g = gram(yh, yl, i, i * BLK, half)
        gf[i * BLK:(i + 1) * BLK, i * BLK:half] = g
        put(gh, gl, i, i * BLK, g)
        sq = g * g
        total = total + 2.0 * jnp.sum(sq) - jnp.sum(sq[:, :BLK])
    load.wait()
    yh[half:, :], yl[half:, :] = split(oth[...])
    turned[:, half:] = oth[:, pl.ds(col, 128)].T
    for i in range(blocks):
        first = max(half, i * BLK)
        g = gram(yh, yl, i, first, n)
        gf[i * BLK:(i + 1) * BLK, first:] = g
        put(gh, gl, i, first, g)
        sq = g * g
        total = total + 2.0 * jnp.sum(sq)
        if i * BLK >= half:
            total = total - jnp.sum(sq[:, :BLK])
    root = lax.rsqrt(jnp.full((8, 128), total + 1e-06, F32))
    f2 = jnp.max(root)
    f1 = jnp.max(jnp.sqrt(root))
    for i in range(blocks):
        at = slice(i * BLK, (i + 1) * BLK), slice(i * BLK, n)
        b = (2.0 * f2) * gf[at] - (f2 * f2) * square(gh, gl, i)
        bf[at] = b
        put(bh, bl, i, i * BLK, b)
    for i in range(blocks):
        at = slice(i * BLK, (i + 1) * BLK), slice(i * BLK, n)
        put(yh, yl, i, i * BLK, 2.0 * bf[at] - square(bh, bl, i))

    first = turned[pl.ds(pl.multiple_of(place_ref[2] * rows, rows), rows), :] * f1
    pair = jnp.concatenate([first, first - f2 * thin(first, gh, gl)], axis=0)
    quad = jnp.concatenate([pair, pair - thin(pair, bh, bl)], axis=0)

    def mix(k):
        terms = [coef[4 * k + q] * quad[q * rows:(q + 1) * rows] for q in range(4) if 4 * k + q < len(coef)]
        return functools.reduce(lambda a, b: a + b, terms)

    u = mix((len(coef) - 1) // 4)
    for k in range((len(coef) - 1) // 4 - 1, -1, -1):
        u = u - thin(u, yh, yl) + mix(k)
    u = u * math.sqrt(n)
    low = place_ref[0] == 0
    out_ref[:, :half] = jnp.where(low, u[:, :half], u[:, half:])
    out_ref[:, half:] = jnp.where(low, u[:, half:], u[:, :half])


def polar(place, own, oth):
    half, n = own.shape
    part, full = pltpu.VMEM((n, n), BF), pltpu.VMEM((n, n), F32)
    return pl.pallas_call(
        functools.partial(polar_kernel, polar_polynomial(ITERS)),
        in_specs=[
            pl.BlockSpec(memory_space=pltpu.SMEM),
            pl.BlockSpec(memory_space=pltpu.VMEM),
            pl.BlockSpec(memory_space=pl.ANY),
        ],
        out_specs=pl.BlockSpec(memory_space=pltpu.VMEM),
        out_shape=jax.ShapeDtypeStruct((32, n), F32),
        scratch_shapes=[pltpu.VMEM((half, n), F32)] + [part] * 6 + [full] * 2
        + [pltpu.VMEM((128, n), F32), pltpu.SemaphoreType.DMA],
        compiler_params=pltpu.CompilerParams(vmem_limit_bytes=40 * MIB),
        name="polar",
    )(place, own, oth)


AXES = ("gx", "gy")
CORES, SIDE, DEPTH = 2, 4, 8


def place_of(y, x, c, z):
    return ((y * SIDE + x) * CORES + c) * DEPTH + z


def ring_pairs(n, odd):
    pairs = [((i + odd) % n, (i + 1 + odd) % n) for i in range(0, n, 2)]
    return [p if k % 2 == 0 else p[::-1] for k, p in enumerate(pairs)]


def cube_groups():
    return [
        [place_of(y, x, c, z) for y in py for x in px for z in pz]
        for c in range(CORES)
        for py in ring_pairs(SIDE, c)
        for px in ring_pairs(SIDE, c)
        for pz in ring_pairs(DEPTH, c)
    ]


def square_groups():
    return [
        [place_of(y, x, c, z) for y in py for x in px]
        for c in range(CORES)
        for py in ring_pairs(SIDE, 1 - c)
        for px in ring_pairs(SIDE, 1 - c)
        for z in range(DEPTH)
    ]


def swap(fn):
    return [
        (place_of(y, x, c, z), place_of(*fn(y, x, c, z)))
        for y in range(SIDE) for x in range(SIDE) for c in range(CORES) for z in range(DEPTH)
    ]


def mate(n, odd):
    table = {}
    for i in range(0, n, 2):
        a, b = (i + odd) % n, (i + 1 + odd) % n
        table[a], table[b] = b, a
    return table


def far(c):
    table = {}
    for a, b in ((0, 3), (4, 7), (2, 5), (6, 1)):
        a, b = (a + c) % DEPTH, (b + c) % DEPTH
        table[a], table[b] = b, a
    return table


SWAP_CORE = swap(lambda y, x, c, z: (y, x, 1 - c, z))
SWAP_Z = swap(lambda y, x, c, z: (y, x, c, mate(DEPTH, 1 - c)[z]))
SWAP_FAR = swap(lambda y, x, c, z: (y, x, c, far(c)[z]))


def send(value, pairs):
    return lax.ppermute(value, AXES, pairs)


def reduce_half(value, bit, pairs):
    half = value.shape[0] // 2
    away = lax.dynamic_slice_in_dim(value, (1 - bit) * half, half, 0)
    keep = lax.dynamic_slice_in_dim(value, bit * half, half, 0)
    return keep + send(away, pairs)


def gather_half(value, bit, pairs):
    other = send(value, pairs)
    return jnp.where(bit == 0, jnp.concatenate([value, other]), jnp.concatenate([other, value]))


def body(corpus, rotation, code_table, codebooks):
    rows, d = corpus.shape
    gx = lax.axis_index("gx")
    core = gx % CORES
    codes_t = code_table.T
    books_t = codebooks.transpose(0, 2, 1)
    held = [pltpu.with_memory_space_constraint(v, pltpu.HBM) for v in (codes_t, books_t, corpus, rotation)]
    scale = 1.0 / math.sqrt(rows * lax.axis_size("gx") * lax.axis_size("gy"))

    far_half, near_half = (1 - core).reshape(1), core.reshape(1)
    far_term, far_words = cross_first(far_half, held[0], held[1], held[2], scale)
    arrived = send(far_term, SWAP_CORE)
    near_term, near_words = cross_first(near_half, held[0], held[1], held[2], scale)

    groups = cube_groups()
    members = len(groups[0])
    summed = (near_term + arrived).reshape(members, -1, d)
    pieces = lax.all_to_all(summed, AXES, 0, 0, axis_index_groups=groups)
    piece = jnp.sum(pieces, axis=0)

    inner = square_groups()
    parts = lax.all_to_all(piece.reshape(len(inner[0]), -1, d), AXES, 0, 0, axis_index_groups=inner)
    part = jnp.sum(parts, axis=0)
    part = part + send(part, SWAP_Z)
    part, far_words = lax.optimization_barrier((part, far_words))
    other = send(part, SWAP_FAR)
    gaps = distortion(far_half, held[3], held[2], far_words)
    other, gaps = lax.optimization_barrier((other, gaps))
    part = part + other
    parts = lax.all_to_all(jnp.broadcast_to(part[None], parts.shape), AXES, 0, 0, axis_index_groups=inner)
    piece = parts.reshape(-1, d)
    own = lax.all_to_all(jnp.broadcast_to(piece[None], (members,) + piece.shape), AXES, 0, 0, axis_index_groups=groups)
    own = own.reshape(-1, d)
    own, near_words = lax.optimization_barrier((own, near_words))
    other = send(own, SWAP_CORE)
    gaps = gaps + distortion(near_half, held[3], held[2], near_words)
    other, gaps = lax.optimization_barrier((other, gaps))
    place = jnp.stack([core, gx // 4, gx % 4])
    return polar(place, own, other), gaps.reshape(rows)


def solution(mesh):
    return jax.shard_map(
        body,
        mesh=mesh,
        in_specs=(P(("gx", "gy"), None), P(), P(("gx", "gy"), None), P()),
        out_specs=(P("gx", None), P(("gx", "gy"))),
        check_vma=False,
    )
```

```python
import math, functools
import numpy as np
import jax, jax.numpy as jnp
from jax import lax
from jax.sharding import PartitionSpec as P
from jax.experimental import pallas as pl
from jax.experimental.pallas import tpu as pltpu

BF, F32 = jnp.bfloat16, jnp.float32
MIB = 1 << 20
BLK = 256
ITERS = 4
CHUNK = 16

def split(x):
    hi = x.astype(BF)
    return hi, (x - hi.astype(F32)).astype(BF)

def nt(a, b):
    return lax.dot_general(a, b, (((1,), (1,)), ((), ())), preferred_element_type=F32)

def nn(a, b):
    return lax.dot_general(a, b, (((1,), (0,)), ((), ())), preferred_element_type=F32)

def rebuild(codes, books, words, block):
    width = books.shape[1]
    word = lax.broadcasted_iota(jnp.int16, (books.shape[2], codes.shape[1]), 0)
    one, zero = jnp.ones((), BF), jnp.zeros((), BF)
    picks = codes[block * CHUNK:(block + 1) * CHUNK, :].astype(jnp.int16)
    for k in range(CHUNK):
        s = block * CHUNK + k
        hot = jnp.where(word == picks[k:k + 1, :], one, zero)
        words[s * width:(s + 1) * width, :] = nn(books[s], hot).astype(BF)


def first_kernel(scale, half_ref, mine_ref, codes_hbm, books_hbm, corpus_hbm, out, words_hbm, codes, books, corpus, words, sems):
    subs = books.shape[0]
    first = pl.multiple_of(half_ref[0] * subs, subs)
    tables = []
    for block in range(subs // CHUNK):
        at, to = pl.ds(first + block * CHUNK, CHUNK), pl.ds(block * CHUNK, CHUNK)
        tables.append(pltpu.make_async_copy(codes_hbm.at[at], codes.at[to], sems.at[2 * block]))
        tables.append(pltpu.make_async_copy(books_hbm.at[at], books.at[to], sems.at[2 * block + 1]))
    whole = pltpu.make_async_copy(corpus_hbm, corpus, sems.at[len(tables)])
    for load in tables + [whole]:
        load.start()
    for block in range(subs // CHUNK):
        tables[2 * block].wait()
        tables[2 * block + 1].wait()
        rebuild(codes, books, words, block)
    store = pltpu.make_async_copy(words, words_hbm, sems.at[len(tables) + 1])
    store.start()
    whole.wait()
    for k in range(corpus.shape[1] // BLK):
        c = slice(k * BLK, (k + 1) * BLK)
        out[:, c] = nn(words[...], corpus[:, c]) * scale
    store.wait()


def cross_half(half, mine, codes_t, books_t, corpus, scale):
    subs, width, size = books_t.shape
    rows, d = corpus.shape
    part = subs // 2
    return pl.pallas_call(
        functools.partial(first_kernel, scale),
        in_specs=[pl.BlockSpec(memory_space=pltpu.SMEM)] * 2 + [pl.BlockSpec(memory_space=pl.ANY)] * 3,
        out_specs=[pl.BlockSpec(memory_space=pltpu.VMEM), pl.BlockSpec(memory_space=pltpu.HBM)],
        out_shape=[jax.ShapeDtypeStruct((part * width, d), F32), pltpu.HBM((part * width, rows), BF)],
        scratch_shapes=[
            pltpu.VMEM((part, rows), jnp.int32),
            pltpu.VMEM((part, width, size), BF),
            pltpu.VMEM((rows, d), BF),
            pltpu.VMEM((part * width, rows), BF),
            pltpu.SemaphoreType.DMA((2 + 2 * (part // CHUNK),)),
        ],
        compiler_params=pltpu.CompilerParams(vmem_limit_bytes=24 * MIB),
        name="cross_half",
    )(half, mine, codes_t, books_t, corpus)


def pick_kernel(mine_ref, pieces_ref, *out_refs):
    rows = out_refs[0].shape[0]
    for k, out_ref in enumerate(out_refs):
        at = pl.ds(pl.multiple_of((mine_ref[0] ^ k) * rows, rows), rows)
        total = pieces_ref[0, at, :]
        for p in range(1, pieces_ref.shape[0]):
            total = total + pieces_ref[p, at, :]
        out_ref[...] = total


def pick(mine, pieces):
    _, rows, d = pieces.shape
    return pl.pallas_call(
        pick_kernel,
        in_specs=[pl.BlockSpec(memory_space=pltpu.SMEM), pl.BlockSpec(memory_space=pltpu.VMEM)],
        out_specs=[pl.BlockSpec(memory_space=pltpu.VMEM)] * 4,
        out_shape=[jax.ShapeDtypeStruct((rows // 4, d), F32)] * 4,
        compiler_params=pltpu.CompilerParams(vmem_limit_bytes=8 * MIB),
        name="pick",
    )(mine, pieces)


def spread_kernel(mine_ref, *refs):
    *part_refs, out_ref = refs
    rows = part_refs[0].shape[0]
    for k, part_ref in enumerate(part_refs):
        at = pl.ds(pl.multiple_of((mine_ref[0] ^ k) * rows, rows), rows)
        for p in range(out_ref.shape[0]):
            out_ref[p, at, :] = part_ref[...]


def spread(mine, parts, members):
    rows, d = parts[0].shape
    return pl.pallas_call(
        spread_kernel,
        in_specs=[pl.BlockSpec(memory_space=pltpu.SMEM)] + [pl.BlockSpec(memory_space=pltpu.VMEM)] * 4,
        out_specs=pl.BlockSpec(memory_space=pltpu.VMEM),
        out_shape=jax.ShapeDtypeStruct((members, 4 * rows, d), F32),
        compiler_params=pltpu.CompilerParams(vmem_limit_bytes=8 * MIB),
        name="spread",
    )(mine, *parts)


def dist_kernel(half_ref, sums_ref, rot_hbm, corpus_hbm, words_hbm, out_ref, rot, corpus, words, sems):
    cols = words.shape[0]
    first = pl.multiple_of(half_ref[0] * cols, cols)
    loads = [
        pltpu.make_async_copy(corpus_hbm, corpus, sems.at[0]),
        pltpu.make_async_copy(rot_hbm.at[:, pl.ds(first, cols)], rot, sems.at[1]),
        pltpu.make_async_copy(words_hbm, words, sems.at[2]),
    ]
    for load in loads:
        load.start()
    for load in loads:
        load.wait()
    rotated = lax.dot_general(rot[...], corpus[...], (((0,), (1,)), ((), ())), preferred_element_type=F32)
    gap = rotated - words[...].astype(F32)
    out_ref[...] = sums_ref[...] + jnp.sum(gap * gap, axis=0, keepdims=True)


def distortion(half, sums, rotation, corpus, words):
    rows, d = corpus.shape
    cols = words.shape[0]
    return pl.pallas_call(
        dist_kernel,
        in_specs=[pl.BlockSpec(memory_space=pltpu.SMEM), pl.BlockSpec(memory_space=pltpu.VMEM)] + [pl.BlockSpec(memory_space=pl.ANY)] * 3,
        out_specs=pl.BlockSpec(memory_space=pltpu.VMEM),
        out_shape=jax.ShapeDtypeStruct((1, rows), F32),
        scratch_shapes=[
            pltpu.VMEM((d, cols), BF),
            pltpu.VMEM((rows, d), BF),
            pltpu.VMEM((cols, rows), BF),
            pltpu.SemaphoreType.DMA((3,)),
        ],
        compiler_params=pltpu.CompilerParams(vmem_limit_bytes=24 * MIB),
        name="distortion",
    )(half, sums, rotation, corpus, words)


def polar_polynomial(steps):
    poly = np.polynomial.polynomial
    e, out = np.array([0.0, 1.0]), np.array([1.0])
    for _ in range(steps):
        out = poly.polymul(out, poly.polyadd([1.0], 0.5 * e))
        sq = poly.polymul(e, e)
        e = poly.polyadd(0.75 * sq, 0.25 * poly.polymul(sq, e))
    return [float(v) for v in out]


def put(hi, lo, i, first, val):
    r = slice(i * BLK, (i + 1) * BLK)
    last = first + val.shape[1]
    hi[r, first:last], lo[r, first:last] = split(val)
    begin = max(first, (i + 1) * BLK)
    if begin < last:
        hi[begin:last, r], lo[begin:last, r] = split(val[:, begin - first:].T)


def inner(hi, lo, i, first, last, mul):
    r, c = slice(i * BLK, (i + 1) * BLK), slice(first, last)

    def times(a, b, at):
        return mul(a[r, :], b[at, :] if mul is nt else b[:, at])

    mixed = times(hi, lo, c)
    if first > i * BLK:
        mixed = mixed + times(lo, hi, c)
    else:
        corner = mixed[:, :BLK] + mixed[:, :BLK].T
        if last > first + BLK:
            rest = mixed[:, BLK:] + times(lo, hi, slice(first + BLK, last))
            mixed = jnp.concatenate([corner, rest], axis=1)
        else:
            mixed = corner
    return times(hi, hi, c) + mixed


def thin(u, hi, lo):
    h, l = split(u)
    m = u.shape[0]
    p = nn(jnp.concatenate([h, l], axis=0), hi[...])
    return p[:m] + (p[m:] + nn(h, lo[...]))


def polar_kernel(coef, place_ref, own_ref, oth_hbm, out_ref, oth, yh, yl, gh, gl, bh, bl, gf, bf, turned, sem):
    n = yh.shape[0]
    half = n // 2
    blocks = n // BLK
    rows = out_ref.shape[0]
    load = pltpu.make_async_copy(oth_hbm, oth, sem)
    load.start()
    col = pl.multiple_of(place_ref[1] * 128, 128)
    yh[:half, :], yl[:half, :] = split(own_ref[...])
    turned[:, :half] = own_ref[:, pl.ds(col, 128)].T
    total = jnp.zeros((), F32)
    for i in range(half // BLK):
        g = inner(yh, yl, i, i * BLK, half, nt)
        gf[i * BLK:(i + 1) * BLK, i * BLK:half] = g
        put(gh, gl, i, i * BLK, g)
        sq = g * g
        total = total + 2.0 * jnp.sum(sq) - jnp.sum(sq[:, :BLK])
    load.wait()
    yh[half:, :], yl[half:, :] = split(oth[...])
    turned[:, half:] = oth[:, pl.ds(col, 128)].T
    for i in range(blocks):
        first = max(half, i * BLK)
        g = inner(yh, yl, i, first, n, nt)
        gf[i * BLK:(i + 1) * BLK, first:] = g
        put(gh, gl, i, first, g)
        sq = g * g
        total = total + 2.0 * jnp.sum(sq)
        if i * BLK >= half:
            total = total - jnp.sum(sq[:, :BLK])
    root = lax.rsqrt(jnp.full((8, 128), total + 1e-06, F32))
    f2 = jnp.max(root)
    f1 = jnp.max(jnp.sqrt(root))
    for i in range(blocks):
        at = slice(i * BLK, (i + 1) * BLK), slice(i * BLK, n)
        b = (2.0 * f2) * gf[at] - (f2 * f2) * inner(gh, gl, i, i * BLK, n, nn)
        bf[at] = b
        put(bh, bl, i, i * BLK, b)
    for i in range(blocks):
        at = slice(i * BLK, (i + 1) * BLK), slice(i * BLK, n)
        put(yh, yl, i, i * BLK, 2.0 * bf[at] - inner(bh, bl, i, i * BLK, n, nn))

    first = turned[pl.ds(pl.multiple_of(place_ref[2] * rows, rows), rows), :] * f1
    pair = jnp.concatenate([first, first - f2 * thin(first, gh, gl)], axis=0)
    quad = jnp.concatenate([pair, pair - thin(pair, bh, bl)], axis=0)

    def mix(k):
        terms = [coef[4 * k + q] * quad[q * rows:(q + 1) * rows] for q in range(4) if 4 * k + q < len(coef)]
        return functools.reduce(lambda a, b: a + b, terms)

    u = mix((len(coef) - 1) // 4)
    for k in range((len(coef) - 1) // 4 - 1, -1, -1):
        u = u - thin(u, yh, yl) + mix(k)
    u = u * math.sqrt(n)
    low = place_ref[0] == 0
    out_ref[:, :half] = jnp.where(low, u[:, :half], u[:, half:])
    out_ref[:, half:] = jnp.where(low, u[:, half:], u[:, :half])


def polar(place, own, oth):
    half, n = own.shape
    part, full = pltpu.VMEM((n, n), BF), pltpu.VMEM((n, n), F32)
    return pl.pallas_call(
        functools.partial(polar_kernel, polar_polynomial(ITERS)),
        in_specs=[
            pl.BlockSpec(memory_space=pltpu.SMEM),
            pl.BlockSpec(memory_space=pltpu.VMEM),
            pl.BlockSpec(memory_space=pl.ANY),
        ],
        out_specs=pl.BlockSpec(memory_space=pltpu.VMEM),
        out_shape=jax.ShapeDtypeStruct((32, n), F32),
        scratch_shapes=[pltpu.VMEM((half, n), F32)] + [part] * 6 + [full] * 2
        + [pltpu.VMEM((128, n), F32), pltpu.SemaphoreType.DMA],
        compiler_params=pltpu.CompilerParams(vmem_limit_bytes=40 * MIB),
        name="polar",
    )(place, own, oth)


AXES = ("gx", "gy")
CORES, SIDE, DEPTH = 2, 4, 8


def place_of(y, x, c, z):
    return ((y * SIDE + x) * CORES + c) * DEPTH + z


def ring_pairs(n, odd):
    pairs = [((i + odd) % n, (i + 1 + odd) % n) for i in range(0, n, 2)]
    return [p if k % 2 == 0 else p[::-1] for k, p in enumerate(pairs)]


def cube_groups():
    return [
        [place_of(y, x, c, z) for y in py for x in px for z in pz]
        for c in range(CORES)
        for py in ring_pairs(SIDE, c)
        for px in ring_pairs(SIDE, c)
        for pz in ring_pairs(DEPTH, c)
    ]


def swap(fn):
    return [
        (place_of(y, x, c, z), place_of(*fn(y, x, c, z)))
        for y in range(SIDE) for x in range(SIDE) for c in range(CORES) for z in range(DEPTH)
    ]


def mate(n, odd):
    table = {}
    for i in range(0, n, 2):
        a, b = (i + odd) % n, (i + 1 + odd) % n
        table[a], table[b] = b, a
    return table


def far(c):
    table = {}
    for a, b in ((0, 3), (4, 7), (2, 5), (6, 1)):
        a, b = (a + c) % DEPTH, (b + c) % DEPTH
        table[a], table[b] = b, a
    return table


SWAP_CORE = swap(lambda y, x, c, z: (y, x, 1 - c, z))
SWAP_Z = swap(lambda y, x, c, z: (y, x, c, mate(DEPTH, 1 - c)[z]))
SWAP_FAR = swap(lambda y, x, c, z: (y, x, c, far(c)[z]))

SWAP_X = swap(lambda y, x, c, z: (y, mate(SIDE, 1 - c)[x], c, z))
SWAP_Y = swap(lambda y, x, c, z: (mate(SIDE, 1 - c)[y], x, c, z))
SWAP_XY = swap(lambda y, x, c, z: (mate(SIDE, 1 - c)[y], mate(SIDE, 1 - c)[x], c, z))

SWAP_BOTH = swap(lambda y, x, c, z: (y, x, c, far(c)[mate(DEPTH, 1 - c)[z]]))


def send(value, pairs):
    return lax.ppermute(value, AXES, pairs)


def reduce_half(value, bit, pairs):
    half = value.shape[0] // 2
    away = lax.dynamic_slice_in_dim(value, (1 - bit) * half, half, 0)
    keep = lax.dynamic_slice_in_dim(value, bit * half, half, 0)
    return keep + send(away, pairs)


def gather_half(value, bit, pairs):
    other = send(value, pairs)
    return jnp.where(bit == 0, jnp.concatenate([value, other]), jnp.concatenate([other, value]))


def body(corpus, rotation, code_table, codebooks):
    rows, d = corpus.shape
    gx = lax.axis_index("gx")
    core = gx % CORES
    mine = (gx // CORES // SIDE % 2 * 2 + gx // CORES % 2).reshape(1)
    codes_t = code_table.T
    books_t = codebooks.transpose(0, 2, 1)
    held = [pltpu.with_memory_space_constraint(v, pltpu.HBM) for v in (codes_t, books_t, corpus, rotation)]
    scale = 1.0 / math.sqrt(rows * lax.axis_size("gx") * lax.axis_size("gy"))

    far_half, near_half = (1 - core).reshape(1), core.reshape(1)
    far_term, far_words = cross_half(far_half, mine, held[0], held[1], held[2], scale)
    arrived = send(far_term, SWAP_CORE)
    near_term, near_words = cross_half(near_half, mine, held[0], held[1], held[2], scale)

    groups = cube_groups()
    members = len(groups[0])
    summed = (near_term + arrived).reshape(members, -1, d)
    pieces = lax.all_to_all(summed, AXES, 0, 0, axis_index_groups=groups)
    part, *away = pick(mine, pieces)
    got = [send(v, p) for v, p in zip(away[::-1], (SWAP_XY, SWAP_Y, SWAP_X))]
    part = part + got[0] + got[1] + got[2]
    part, far_words = lax.optimization_barrier((part, far_words))
    others = [send(part, pairs) for pairs in (SWAP_BOTH, SWAP_FAR, SWAP_Z)]
    gaps = distortion(far_half, jnp.zeros((1, rows), F32), held[3], held[2], far_words)
    others, gaps = lax.optimization_barrier((others, gaps))
    part = part + others[0] + others[1] + others[2]
    got = [send(part, p) for p in (SWAP_XY, SWAP_Y, SWAP_X)]
    gathered = spread(mine, [part] + got[::-1], members)
    own = lax.all_to_all(gathered, AXES, 0, 0, axis_index_groups=groups)
    own = own.reshape(-1, d)
    own, near_words = lax.optimization_barrier((own, near_words))
    other = send(own, SWAP_CORE)
    gaps = distortion(near_half, gaps, held[3], held[2], near_words)
    other, gaps = lax.optimization_barrier((other, gaps))
    place = jnp.stack([core, gx // 4, gx % 4])
    return polar(place, own, other), gaps.reshape(rows)


def solution(mesh):
    return jax.shard_map(
        body,
        mesh=mesh,
        in_specs=(P(("gx", "gy"), None), P(), P(("gx", "gy"), None), P()),
        out_specs=(P("gx", None), P(("gx", "gy"))),
        check_vma=False,
    )
```

```python
import math, functools
import numpy as np
import jax, jax.numpy as jnp
from jax import lax
from jax.sharding import PartitionSpec as P
from jax.experimental import pallas as pl
from jax.experimental.pallas import tpu as pltpu

BF, F32 = jnp.bfloat16, jnp.float32
MIB = 1 << 20
BLK = 256
ITERS = 4
CHUNK = 16

def split(x):
    hi = x.astype(BF)
    return hi, (x - hi.astype(F32)).astype(BF)

def nt(a, b):
    return lax.dot_general(a, b, (((1,), (1,)), ((), ())), preferred_element_type=F32)

def nn(a, b):
    return lax.dot_general(a, b, (((1,), (0,)), ((), ())), preferred_element_type=F32)

def rebuild(codes, books, words, block):
    width = books.shape[1]
    word = lax.broadcasted_iota(jnp.int16, (books.shape[2], codes.shape[1]), 0)
    one, zero = jnp.ones((), BF), jnp.zeros((), BF)
    picks = codes[block * CHUNK:(block + 1) * CHUNK, :].astype(jnp.int16)
    for k in range(CHUNK):
        s = block * CHUNK + k
        hot = jnp.where(word == picks[k:k + 1, :], one, zero)
        words[s * width:(s + 1) * width, :] = nn(books[s], hot).astype(BF)


def first_kernel(scale, half_ref, mine_ref, codes_hbm, books_hbm, corpus_hbm, out, words_hbm, codes, books, corpus, words, sems):
    subs = books.shape[0]
    first = pl.multiple_of(half_ref[0] * subs, subs)
    tables = []
    for block in range(subs // CHUNK):
        at, to = pl.ds(first + block * CHUNK, CHUNK), pl.ds(block * CHUNK, CHUNK)
        tables.append(pltpu.make_async_copy(codes_hbm.at[at], codes.at[to], sems.at[2 * block]))
        tables.append(pltpu.make_async_copy(books_hbm.at[at], books.at[to], sems.at[2 * block + 1]))
    whole = pltpu.make_async_copy(corpus_hbm, corpus, sems.at[len(tables)])
    for load in tables + [whole]:
        load.start()
    for block in range(subs // CHUNK):
        tables[2 * block].wait()
        tables[2 * block + 1].wait()
        rebuild(codes, books, words, block)
    store = pltpu.make_async_copy(words, words_hbm, sems.at[len(tables) + 1])
    store.start()
    whole.wait()
    for k in range(corpus.shape[1] // BLK):
        c = slice(k * BLK, (k + 1) * BLK)
        out[:, c] = nn(words[...], corpus[:, c]) * scale
    store.wait()


def cross_half(half, mine, codes_t, books_t, corpus, scale):
    subs, width, size = books_t.shape
    rows, d = corpus.shape
    part = subs // 2
    return pl.pallas_call(
        functools.partial(first_kernel, scale),
        in_specs=[pl.BlockSpec(memory_space=pltpu.SMEM)] * 2 + [pl.BlockSpec(memory_space=pl.ANY)] * 3,
        out_specs=[pl.BlockSpec(memory_space=pltpu.VMEM), pl.BlockSpec(memory_space=pltpu.HBM)],
        out_shape=[jax.ShapeDtypeStruct((part * width, d), F32), pltpu.HBM((part * width, rows), BF)],
        scratch_shapes=[
            pltpu.VMEM((part, rows), jnp.int32),
            pltpu.VMEM((part, width, size), BF),
            pltpu.VMEM((rows, d), BF),
            pltpu.VMEM((part * width, rows), BF),
            pltpu.SemaphoreType.DMA((2 + 2 * (part // CHUNK),)),
        ],
        compiler_params=pltpu.CompilerParams(vmem_limit_bytes=24 * MIB),
        name="cross_half",
    )(half, mine, codes_t, books_t, corpus)


def second_kernel(scale, half_ref, codes_ref, books_ref, corpus_ref, out_ref, words_hbm, words, sem):
    subs = books_ref.shape[0] // 2
    first = pl.multiple_of(half_ref[0] * subs, subs)
    at = pl.ds(first, subs)
    for block in range(subs // CHUNK):
        rebuild(codes_ref.at[at], books_ref.at[at], words, block)
    store = pltpu.make_async_copy(words, words_hbm, sem)
    store.start()
    for k in range(corpus_ref.shape[1] // BLK):
        c = slice(k * BLK, (k + 1) * BLK)
        out_ref[:, c] = nn(words[...], corpus_ref[:, c]) * scale
    store.wait()


def cross_second(half, codes_t, books_t, corpus, scale):
    subs, width, _ = books_t.shape
    rows, d = corpus.shape
    part = subs // 2
    return pl.pallas_call(
        functools.partial(second_kernel, scale),
        in_specs=[pl.BlockSpec(memory_space=pltpu.SMEM)] + [pl.BlockSpec(memory_space=pltpu.VMEM)] * 3,
        out_specs=[pl.BlockSpec(memory_space=pltpu.VMEM), pl.BlockSpec(memory_space=pltpu.HBM)],
        out_shape=[jax.ShapeDtypeStruct((part * width, d), F32), pltpu.HBM((part * width, rows), BF)],
        scratch_shapes=[pltpu.VMEM((part * width, rows), BF), pltpu.SemaphoreType.DMA],
        compiler_params=pltpu.CompilerParams(vmem_limit_bytes=16 * MIB),
        name="cross_second",
    )(half, codes_t, books_t, corpus)


def pick_kernel(mine_ref, pieces_ref, *out_refs):
    rows = out_refs[0].shape[0]
    for k, out_ref in enumerate(out_refs):
        at = pl.ds(pl.multiple_of((mine_ref[0] ^ k) * rows, rows), rows)
        total = pieces_ref[0, at, :]
        for p in range(1, pieces_ref.shape[0]):
            total = total + pieces_ref[p, at, :]
        out_ref[...] = total


def pick(mine, pieces):
    _, rows, d = pieces.shape
    return pl.pallas_call(
        pick_kernel,
        in_specs=[pl.BlockSpec(memory_space=pltpu.SMEM), pl.BlockSpec(memory_space=pltpu.VMEM)],
        out_specs=[pl.BlockSpec(memory_space=pltpu.VMEM)] * 4,
        out_shape=[jax.ShapeDtypeStruct((rows // 4, d), F32)] * 4,
        compiler_params=pltpu.CompilerParams(vmem_limit_bytes=8 * MIB),
        name="pick",
    )(mine, pieces)


def spread_kernel(mine_ref, *refs):
    *part_refs, out_ref = refs
    rows = part_refs[0].shape[0]
    for k, part_ref in enumerate(part_refs):
        at = pl.ds(pl.multiple_of((mine_ref[0] ^ k) * rows, rows), rows)
        for p in range(out_ref.shape[0]):
            out_ref[p, at, :] = part_ref[...]


def spread(mine, parts, members):
    rows, d = parts[0].shape
    return pl.pallas_call(
        spread_kernel,
        in_specs=[pl.BlockSpec(memory_space=pltpu.SMEM)] + [pl.BlockSpec(memory_space=pltpu.VMEM)] * 4,
        out_specs=pl.BlockSpec(memory_space=pltpu.VMEM),
        out_shape=jax.ShapeDtypeStruct((members, 4 * rows, d), F32),
        compiler_params=pltpu.CompilerParams(vmem_limit_bytes=8 * MIB),
        name="spread",
    )(mine, *parts)


def dist_kernel(half_ref, sums_ref, rot_hbm, corpus_hbm, words_hbm, out_ref, rot, corpus, words, sems):
    cols = words.shape[0]
    first = pl.multiple_of(half_ref[0] * cols, cols)
    loads = [
        pltpu.make_async_copy(corpus_hbm, corpus, sems.at[0]),
        pltpu.make_async_copy(rot_hbm.at[:, pl.ds(first, cols)], rot, sems.at[1]),
        pltpu.make_async_copy(words_hbm, words, sems.at[2]),
    ]
    for load in loads:
        load.start()
    for load in loads:
        load.wait()
    rotated = lax.dot_general(rot[...], corpus[...], (((0,), (1,)), ((), ())), preferred_element_type=F32)
    gap = rotated - words[...].astype(F32)
    out_ref[...] = sums_ref[...] + jnp.sum(gap * gap, axis=0, keepdims=True)


def distortion(half, sums, rotation, corpus, words):
    rows, d = corpus.shape
    cols = words.shape[0]
    return pl.pallas_call(
        dist_kernel,
        in_specs=[pl.BlockSpec(memory_space=pltpu.SMEM), pl.BlockSpec(memory_space=pltpu.VMEM)] + [pl.BlockSpec(memory_space=pl.ANY)] * 3,
        out_specs=pl.BlockSpec(memory_space=pltpu.VMEM),
        out_shape=jax.ShapeDtypeStruct((1, rows), F32),
        scratch_shapes=[
            pltpu.VMEM((d, cols), BF),
            pltpu.VMEM((rows, d), BF),
            pltpu.VMEM((cols, rows), BF),
            pltpu.SemaphoreType.DMA((3,)),
        ],
        compiler_params=pltpu.CompilerParams(vmem_limit_bytes=24 * MIB),
        name="distortion",
    )(half, sums, rotation, corpus, words)


def polar_polynomial(steps):
    poly = np.polynomial.polynomial
    e, out = np.array([0.0, 1.0]), np.array([1.0])
    for _ in range(steps):
        out = poly.polymul(out, poly.polyadd([1.0], 0.5 * e))
        sq = poly.polymul(e, e)
        e = poly.polyadd(0.75 * sq, 0.25 * poly.polymul(sq, e))
    return [float(v) for v in out]


def put(hi, lo, i, first, val):
    r = slice(i * BLK, (i + 1) * BLK)
    last = first + val.shape[1]
    hi[r, first:last], lo[r, first:last] = split(val)
    begin = max(first, (i + 1) * BLK)
    if begin < last:
        hi[begin:last, r], lo[begin:last, r] = split(val[:, begin - first:].T)


def inner(hi, lo, i, first, last, mul):
    r, c = slice(i * BLK, (i + 1) * BLK), slice(first, last)

    def times(a, b, at):
        return mul(a[r, :], b[at, :] if mul is nt else b[:, at])

    mixed = times(hi, lo, c)
    if first > i * BLK:
        mixed = mixed + times(lo, hi, c)
    else:
        corner = mixed[:, :BLK] + mixed[:, :BLK].T
        if last > first + BLK:
            rest = mixed[:, BLK:] + times(lo, hi, slice(first + BLK, last))
            mixed = jnp.concatenate([corner, rest], axis=1)
        else:
            mixed = corner
    return times(hi, hi, c) + mixed


def thin(u, hi, lo):
    h, l = split(u)
    m = u.shape[0]
    p = nn(jnp.concatenate([h, l], axis=0), hi[...])
    return p[:m] + (p[m:] + nn(h, lo[...]))


def polar_kernel(coef, place_ref, own_ref, oth_hbm, out_ref, oth, yh, yl, gh, gl, bh, bl, gf, bf, turned, sem):
    n = yh.shape[0]
    half = n // 2
    blocks = n // BLK
    rows = out_ref.shape[0]
    load = pltpu.make_async_copy(oth_hbm, oth, sem)
    load.start()
    col = pl.multiple_of(place_ref[1] * 128, 128)
    yh[:half, :], yl[:half, :] = split(own_ref[...])
    turned[:, :half] = own_ref[:, pl.ds(col, 128)].T
    total = jnp.zeros((), F32)
    for i in range(half // BLK):
        g = inner(yh, yl, i, i * BLK, half, nt)
        gf[i * BLK:(i + 1) * BLK, i * BLK:half] = g
        put(gh, gl, i, i * BLK, g)
        sq = g * g
        total = total + 2.0 * jnp.sum(sq) - jnp.sum(sq[:, :BLK])
    load.wait()
    yh[half:, :], yl[half:, :] = split(oth[...])
    turned[:, half:] = oth[:, pl.ds(col, 128)].T
    for i in range(blocks):
        first = max(half, i * BLK)
        g = inner(yh, yl, i, first, n, nt)
        gf[i * BLK:(i + 1) * BLK, first:] = g
        put(gh, gl, i, first, g)
        sq = g * g
        total = total + 2.0 * jnp.sum(sq)
        if i * BLK >= half:
            total = total - jnp.sum(sq[:, :BLK])
    root = lax.rsqrt(jnp.full((8, 128), total + 1e-06, F32))
    f2 = jnp.max(root)
    f1 = jnp.max(jnp.sqrt(root))
    for i in range(blocks):
        at = slice(i * BLK, (i + 1) * BLK), slice(i * BLK, n)
        b = (2.0 * f2) * gf[at] - (f2 * f2) * inner(gh, gl, i, i * BLK, n, nn)
        bf[at] = b
        put(bh, bl, i, i * BLK, b)
    for i in range(blocks):
        at = slice(i * BLK, (i + 1) * BLK), slice(i * BLK, n)
        put(yh, yl, i, i * BLK, 2.0 * bf[at] - inner(bh, bl, i, i * BLK, n, nn))

    first = turned[pl.ds(pl.multiple_of(place_ref[2] * rows, rows), rows), :] * f1
    pair = jnp.concatenate([first, first - f2 * thin(first, gh, gl)], axis=0)
    quad = jnp.concatenate([pair, pair - thin(pair, bh, bl)], axis=0)

    def mix(k):
        terms = [coef[4 * k + q] * quad[q * rows:(q + 1) * rows] for q in range(4) if 4 * k + q < len(coef)]
        return functools.reduce(lambda a, b: a + b, terms)

    u = mix((len(coef) - 1) // 4)
    for k in range((len(coef) - 1) // 4 - 1, -1, -1):
        u = u - thin(u, yh, yl) + mix(k)
    u = u * math.sqrt(n)
    low = place_ref[0] == 0
    out_ref[:, :half] = jnp.where(low, u[:, :half], u[:, half:])
    out_ref[:, half:] = jnp.where(low, u[:, half:], u[:, :half])


def polar(place, own, oth):
    half, n = own.shape
    part, full = pltpu.VMEM((n, n), BF), pltpu.VMEM((n, n), F32)
    return pl.pallas_call(
        functools.partial(polar_kernel, polar_polynomial(ITERS)),
        in_specs=[
            pl.BlockSpec(memory_space=pltpu.SMEM),
            pl.BlockSpec(memory_space=pltpu.VMEM),
            pl.BlockSpec(memory_space=pl.ANY),
        ],
        out_specs=pl.BlockSpec(memory_space=pltpu.VMEM),
        out_shape=jax.ShapeDtypeStruct((32, n), F32),
        scratch_shapes=[pltpu.VMEM((half, n), F32)] + [part] * 6 + [full] * 2
        + [pltpu.VMEM((128, n), F32), pltpu.SemaphoreType.DMA],
        compiler_params=pltpu.CompilerParams(vmem_limit_bytes=40 * MIB),
        name="polar",
    )(place, own, oth)


AXES = ("gx", "gy")
CORES, SIDE, DEPTH = 2, 4, 8


def place_of(y, x, c, z):
    return ((y * SIDE + x) * CORES + c) * DEPTH + z


def ring_pairs(n, odd):
    pairs = [((i + odd) % n, (i + 1 + odd) % n) for i in range(0, n, 2)]
    return [p if k % 2 == 0 else p[::-1] for k, p in enumerate(pairs)]


def cube_groups():
    return [
        [place_of(y, x, c, z) for y in py for x in px for z in pz]
        for c in range(CORES)
        for py in ring_pairs(SIDE, c)
        for px in ring_pairs(SIDE, c)
        for pz in ring_pairs(DEPTH, c)
    ]


def swap(fn):
    return [
        (place_of(y, x, c, z), place_of(*fn(y, x, c, z)))
        for y in range(SIDE) for x in range(SIDE) for c in range(CORES) for z in range(DEPTH)
    ]


def mate(n, odd):
    table = {}
    for i in range(0, n, 2):
        a, b = (i + odd) % n, (i + 1 + odd) % n
        table[a], table[b] = b, a
    return table


def far(c):
    table = {}
    for a, b in ((0, 3), (4, 7), (2, 5), (6, 1)):
        a, b = (a + c) % DEPTH, (b + c) % DEPTH
        table[a], table[b] = b, a
    return table


SWAP_CORE = swap(lambda y, x, c, z: (y, x, 1 - c, z))
SWAP_Z = swap(lambda y, x, c, z: (y, x, c, mate(DEPTH, 1 - c)[z]))
SWAP_FAR = swap(lambda y, x, c, z: (y, x, c, far(c)[z]))

SWAP_X = swap(lambda y, x, c, z: (y, mate(SIDE, 1 - c)[x], c, z))
SWAP_Y = swap(lambda y, x, c, z: (mate(SIDE, 1 - c)[y], x, c, z))
SWAP_XY = swap(lambda y, x, c, z: (mate(SIDE, 1 - c)[y], mate(SIDE, 1 - c)[x], c, z))

SWAP_BOTH = swap(lambda y, x, c, z: (y, x, c, far(c)[mate(DEPTH, 1 - c)[z]]))


def send(value, pairs):
    return lax.ppermute(value, AXES, pairs)


def reduce_half(value, bit, pairs):
    half = value.shape[0] // 2
    away = lax.dynamic_slice_in_dim(value, (1 - bit) * half, half, 0)
    keep = lax.dynamic_slice_in_dim(value, bit * half, half, 0)
    return keep + send(away, pairs)


def gather_half(value, bit, pairs):
    other = send(value, pairs)
    return jnp.where(bit == 0, jnp.concatenate([value, other]), jnp.concatenate([other, value]))


def body(corpus, rotation, code_table, codebooks):
    rows, d = corpus.shape
    gx = lax.axis_index("gx")
    core = gx % CORES
    mine = (gx // CORES // SIDE % 2 * 2 + gx // CORES % 2).reshape(1)
    codes_t = code_table.T
    books_t = codebooks.transpose(0, 2, 1)
    held = [pltpu.with_memory_space_constraint(v, pltpu.HBM) for v in (codes_t, books_t, corpus, rotation)]
    scale = 1.0 / math.sqrt(rows * lax.axis_size("gx") * lax.axis_size("gy"))

    far_half, near_half = (1 - core).reshape(1), core.reshape(1)
    far_term, far_words = cross_half(far_half, mine, held[0], held[1], held[2], scale)
    arrived = send(far_term, SWAP_CORE)
    near_term, near_words = cross_second(near_half, codes_t, books_t, corpus, scale)

    groups = cube_groups()
    members = len(groups[0])
    summed = (near_term + arrived).reshape(members, -1, d)
    pieces = lax.all_to_all(summed, AXES, 0, 0, axis_index_groups=groups)
    part, *away = pick(mine, pieces)
    got = [send(v, p) for v, p in zip(away[::-1], (SWAP_XY, SWAP_Y, SWAP_X))]
    part = part + got[0] + got[1] + got[2]
    part, far_words = lax.optimization_barrier((part, far_words))
    others = [send(part, pairs) for pairs in (SWAP_BOTH, SWAP_FAR, SWAP_Z)]
    gaps = distortion(far_half, jnp.zeros((1, rows), F32), held[3], held[2], far_words)
    others, gaps = lax.optimization_barrier((others, gaps))
    part = part + others[0] + others[1] + others[2]
    got = [send(part, p) for p in (SWAP_XY, SWAP_Y, SWAP_X)]
    gathered = spread(mine, [part] + got[::-1], members)
    own = lax.all_to_all(gathered, AXES, 0, 0, axis_index_groups=groups)
    own = own.reshape(-1, d)
    own, near_words = lax.optimization_barrier((own, near_words))
    other = send(own, SWAP_CORE)
    gaps = distortion(near_half, gaps, held[3], held[2], near_words)
    other, gaps = lax.optimization_barrier((other, gaps))
    place = jnp.stack([core, gx // 4, gx % 4])
    return polar(place, own, other), gaps.reshape(rows)


def solution(mesh):
    return jax.shard_map(
        body,
        mesh=mesh,
        in_specs=(P(("gx", "gy"), None), P(), P(("gx", "gy"), None), P()),
        out_specs=(P("gx", None), P(("gx", "gy"))),
        check_vma=False,
    )
```

```python
import math, functools
import numpy as np
import jax, jax.numpy as jnp
from jax import lax
from jax.sharding import PartitionSpec as P
from jax.experimental import pallas as pl
from jax.experimental.pallas import tpu as pltpu

BF, F32 = jnp.bfloat16, jnp.float32
MIB = 1 << 20
BLK = 256
COARSE = 5
ITERS = 4
CHUNK = 16

def split(x):
    hi = x.astype(BF)
    return hi, (x - hi.astype(F32)).astype(BF)

def nt(a, b):
    return lax.dot_general(a, b, (((1,), (1,)), ((), ())), preferred_element_type=F32)

def nn(a, b):
    return lax.dot_general(a, b, (((1,), (0,)), ((), ())), preferred_element_type=F32)

def rebuild(codes, books, words, block):
    width = books.shape[1]
    word = lax.broadcasted_iota(jnp.int16, (books.shape[2], codes.shape[1]), 0)
    one, zero = jnp.ones((), BF), jnp.zeros((), BF)
    picks = codes[block * CHUNK:(block + 1) * CHUNK, :].astype(jnp.int16)
    for k in range(CHUNK):
        s = block * CHUNK + k
        hot = jnp.where(word == picks[k:k + 1, :], one, zero)
        words[s * width:(s + 1) * width, :] = nn(books[s], hot).astype(BF)


def first_kernel(scale, half_ref, mine_ref, codes_hbm, books_hbm, corpus_hbm, out, words_hbm, codes, books, corpus, words, sems):
    subs = books.shape[0]
    first = pl.multiple_of(half_ref[0] * subs, subs)
    tables = []
    for block in range(subs // CHUNK):
        at, to = pl.ds(first + block * CHUNK, CHUNK), pl.ds(block * CHUNK, CHUNK)
        tables.append(pltpu.make_async_copy(codes_hbm.at[at], codes.at[to], sems.at[2 * block]))
        tables.append(pltpu.make_async_copy(books_hbm.at[at], books.at[to], sems.at[2 * block + 1]))
    whole = pltpu.make_async_copy(corpus_hbm, corpus, sems.at[len(tables)])
    for load in tables + [whole]:
        load.start()
    for block in range(subs // CHUNK):
        tables[2 * block].wait()
        tables[2 * block + 1].wait()
        rebuild(codes, books, words, block)
    store = pltpu.make_async_copy(words, words_hbm, sems.at[len(tables) + 1])
    store.start()
    whole.wait()
    for k in range(corpus.shape[1] // BLK):
        c = slice(k * BLK, (k + 1) * BLK)
        out[:, c] = nn(words[...], corpus[:, c]) * scale
    store.wait()


def cross_half(half, mine, codes_t, books_t, corpus, scale):
    subs, width, size = books_t.shape
    rows, d = corpus.shape
    part = subs // 2
    return pl.pallas_call(
        functools.partial(first_kernel, scale),
        in_specs=[pl.BlockSpec(memory_space=pltpu.SMEM)] * 2 + [pl.BlockSpec(memory_space=pl.ANY)] * 3,
        out_specs=[pl.BlockSpec(memory_space=pltpu.VMEM), pl.BlockSpec(memory_space=pltpu.HBM)],
        out_shape=[jax.ShapeDtypeStruct((part * width, d), F32), pltpu.HBM((part * width, rows), BF)],
        scratch_shapes=[
            pltpu.VMEM((part, rows), jnp.int32),
            pltpu.VMEM((part, width, size), BF),
            pltpu.VMEM((rows, d), BF),
            pltpu.VMEM((part * width, rows), BF),
            pltpu.SemaphoreType.DMA((2 + 2 * (part // CHUNK),)),
        ],
        compiler_params=pltpu.CompilerParams(vmem_limit_bytes=24 * MIB),
        name="cross_half",
    )(half, mine, codes_t, books_t, corpus)


def second_kernel(scale, half_ref, codes_ref, books_ref, corpus_ref, out_ref, words_hbm, words, sem):
    subs = books_ref.shape[0] // 2
    first = pl.multiple_of(half_ref[0] * subs, subs)
    at = pl.ds(first, subs)
    for block in range(subs // CHUNK):
        rebuild(codes_ref.at[at], books_ref.at[at], words, block)
    store = pltpu.make_async_copy(words, words_hbm, sem)
    store.start()
    for k in range(corpus_ref.shape[1] // BLK):
        c = slice(k * BLK, (k + 1) * BLK)
        out_ref[:, c] = nn(words[...], corpus_ref[:, c]) * scale
    store.wait()


def cross_second(half, codes_t, books_t, corpus, scale):
    subs, width, _ = books_t.shape
    rows, d = corpus.shape
    part = subs // 2
    return pl.pallas_call(
        functools.partial(second_kernel, scale),
        in_specs=[pl.BlockSpec(memory_space=pltpu.SMEM)] + [pl.BlockSpec(memory_space=pltpu.VMEM)] * 3,
        out_specs=[pl.BlockSpec(memory_space=pltpu.VMEM), pl.BlockSpec(memory_space=pltpu.HBM)],
        out_shape=[jax.ShapeDtypeStruct((part * width, d), F32), pltpu.HBM((part * width, rows), BF)],
        scratch_shapes=[pltpu.VMEM((part * width, rows), BF), pltpu.SemaphoreType.DMA],
        compiler_params=pltpu.CompilerParams(vmem_limit_bytes=16 * MIB),
        name="cross_second",
    )(half, codes_t, books_t, corpus)


def pick_kernel(mine_ref, pieces_ref, *out_refs):
    rows = out_refs[0].shape[0]
    for k, out_ref in enumerate(out_refs):
        at = pl.ds(pl.multiple_of((mine_ref[0] ^ k) * rows, rows), rows)
        total = pieces_ref[0, at, :]
        for p in range(1, pieces_ref.shape[0]):
            total = total + pieces_ref[p, at, :]
        out_ref[...] = total


def pick(mine, pieces):
    _, rows, d = pieces.shape
    return pl.pallas_call(
        pick_kernel,
        in_specs=[pl.BlockSpec(memory_space=pltpu.SMEM), pl.BlockSpec(memory_space=pltpu.VMEM)],
        out_specs=[pl.BlockSpec(memory_space=pltpu.VMEM)] * 4,
        out_shape=[jax.ShapeDtypeStruct((rows // 4, d), F32)] * 4,
        compiler_params=pltpu.CompilerParams(vmem_limit_bytes=8 * MIB),
        name="pick",
    )(mine, pieces)


def spread_kernel(mine_ref, *refs):
    *part_refs, out_ref = refs
    rows = part_refs[0].shape[0]
    for k, part_ref in enumerate(part_refs):
        at = pl.ds(pl.multiple_of((mine_ref[0] ^ k) * rows, rows), rows)
        for p in range(out_ref.shape[0]):
            out_ref[p, at, :] = part_ref[...]


def spread(mine, parts, members):
    rows, d = parts[0].shape
    return pl.pallas_call(
        spread_kernel,
        in_specs=[pl.BlockSpec(memory_space=pltpu.SMEM)] + [pl.BlockSpec(memory_space=pltpu.VMEM)] * 4,
        out_specs=pl.BlockSpec(memory_space=pltpu.VMEM),
        out_shape=jax.ShapeDtypeStruct((members, 4 * rows, d), F32),
        compiler_params=pltpu.CompilerParams(vmem_limit_bytes=8 * MIB),
        name="spread",
    )(mine, *parts)


def dist_kernel(half_ref, sums_ref, rot_hbm, corpus_hbm, words_hbm, out_ref, rot, corpus, words, sems):
    cols = words.shape[0]
    first = pl.multiple_of(half_ref[0] * cols, cols)
    loads = [
        pltpu.make_async_copy(corpus_hbm, corpus, sems.at[0]),
        pltpu.make_async_copy(rot_hbm.at[:, pl.ds(first, cols)], rot, sems.at[1]),
        pltpu.make_async_copy(words_hbm, words, sems.at[2]),
    ]
    for load in loads:
        load.start()
    for load in loads:
        load.wait()
    rotated = lax.dot_general(rot[...], corpus[...], (((0,), (1,)), ((), ())), preferred_element_type=F32)
    gap = rotated - words[...].astype(F32)
    out_ref[...] = sums_ref[...] + jnp.sum(gap * gap, axis=0, keepdims=True)


def distortion(half, sums, rotation, corpus, words):
    rows, d = corpus.shape
    cols = words.shape[0]
    return pl.pallas_call(
        dist_kernel,
        in_specs=[pl.BlockSpec(memory_space=pltpu.SMEM), pl.BlockSpec(memory_space=pltpu.VMEM)] + [pl.BlockSpec(memory_space=pl.ANY)] * 3,
        out_specs=pl.BlockSpec(memory_space=pltpu.VMEM),
        out_shape=jax.ShapeDtypeStruct((1, rows), F32),
        scratch_shapes=[
            pltpu.VMEM((d, cols), BF),
            pltpu.VMEM((rows, d), BF),
            pltpu.VMEM((cols, rows), BF),
            pltpu.SemaphoreType.DMA((3,)),
        ],
        compiler_params=pltpu.CompilerParams(vmem_limit_bytes=24 * MIB),
        name="distortion",
    )(half, sums, rotation, corpus, words)


def polar_polynomial(steps):
    poly = np.polynomial.polynomial
    e, out = np.array([0.0, 1.0]), np.array([1.0])
    for _ in range(steps):
        out = poly.polymul(out, poly.polyadd([1.0], 0.5 * e))
        sq = poly.polymul(e, e)
        e = poly.polyadd(0.75 * sq, 0.25 * poly.polymul(sq, e))
    return [float(v) for v in out]


def put(hi, lo, i, first, val):
    r = slice(i * BLK, (i + 1) * BLK)
    last = first + val.shape[1]
    hi[r, first:last], lo[r, first:last] = split(val)
    begin = max(first, (i + 1) * BLK)
    if begin < last:
        hi[begin:last, r], lo[begin:last, r] = split(val[:, begin - first:].T)


def inner(hi, lo, i, first, last, mul):
    r, c = slice(i * BLK, (i + 1) * BLK), slice(first, last)

    def times(a, b, at):
        return mul(a[r, :], b[at, :] if mul is nt else b[:, at])

    mixed = times(hi, lo, c)
    if first > i * BLK:
        mixed = mixed + times(lo, hi, c)
    else:
        corner = mixed[:, :BLK] + mixed[:, :BLK].T
        if last > first + BLK:
            rest = mixed[:, BLK:] + times(lo, hi, slice(first + BLK, last))
            mixed = jnp.concatenate([corner, rest], axis=1)
        else:
            mixed = corner
    return times(hi, hi, c) + mixed


def thin(u, hi, lo):
    h, l = split(u)
    m = u.shape[0]
    p = nn(jnp.concatenate([h, l], axis=0), hi[...])
    return p[:m] + (p[m:] + nn(h, lo[...]))


def polar_kernel(coef, place_ref, own_ref, oth_hbm, out_ref, oth, yh, yl, gh, gl, bh, bl, gf, bf, turned, sem):
    n = yh.shape[0]
    half = n // 2
    blocks = n // BLK
    rows = out_ref.shape[0]
    load = pltpu.make_async_copy(oth_hbm, oth, sem)
    load.start()
    col = pl.multiple_of(place_ref[1] * 128, 128)
    yh[:half, :], yl[:half, :] = split(own_ref[...])
    turned[:, :half] = own_ref[:, pl.ds(col, 128)].T
    total = jnp.zeros((), F32)
    for i in range(half // BLK):
        g = inner(yh, yl, i, i * BLK, half, nt)
        gf[i * BLK:(i + 1) * BLK, i * BLK:half] = g
        put(gh, gl, i, i * BLK, g)
        sq = g * g
        total = total + 2.0 * jnp.sum(sq) - jnp.sum(sq[:, :BLK])
    load.wait()
    yh[half:, :], yl[half:, :] = split(oth[...])
    turned[:, half:] = oth[:, pl.ds(col, 128)].T
    for i in range(blocks):
        first = max(half, i * BLK)
        g = inner(yh, yl, i, first, n, nt)
        gf[i * BLK:(i + 1) * BLK, first:] = g
        put(gh, gl, i, first, g)
        sq = g * g
        total = total + 2.0 * jnp.sum(sq)
        if i * BLK >= half:
            total = total - jnp.sum(sq[:, :BLK])
    root = lax.rsqrt(jnp.full((8, 128), total + 1e-06, F32))
    f2 = jnp.max(root)
    f1 = jnp.max(jnp.sqrt(root))
    for i in range(blocks):
        at = slice(i * BLK, (i + 1) * BLK), slice(i * BLK, n)
        b = (2.0 * f2) * gf[at] - (f2 * f2) * inner(gh, gl, i, i * BLK, n, nn)
        bf[at] = b
        put(bh, bl, i, i * BLK, b)
    for i in range(blocks):
        at = slice(i * BLK, (i + 1) * BLK), slice(i * BLK, n)
        put(yh, yl, i, i * BLK, 2.0 * bf[at] - inner(bh, bl, i, i * BLK, n, nn))

    first = turned[pl.ds(pl.multiple_of(place_ref[2] * rows, rows), rows), :] * f1
    pair = jnp.concatenate([first, first - f2 * thin(first, gh, gl)], axis=0)
    quad = jnp.concatenate([pair, pair - thin(pair, bh, bl)], axis=0)

    def mix(k):
        terms = [coef[4 * k + q] * quad[q * rows:(q + 1) * rows] for q in range(4) if 4 * k + q < len(coef)]
        return functools.reduce(lambda a, b: a + b, terms)

    u = mix((len(coef) - 1) // 4)
    for k in range((len(coef) - 1) // 4 - 1, -1, -1):
        step = nn(u.astype(BF), yh[...]) if k >= COARSE else thin(u, yh, yl)
        u = u - step + mix(k)
    u = u * math.sqrt(n)
    low = place_ref[0] == 0
    out_ref[:, :half] = jnp.where(low, u[:, :half], u[:, half:])
    out_ref[:, half:] = jnp.where(low, u[:, half:], u[:, :half])


def polar(place, own, oth):
    half, n = own.shape
    part, full = pltpu.VMEM((n, n), BF), pltpu.VMEM((n, n), F32)
    return pl.pallas_call(
        functools.partial(polar_kernel, polar_polynomial(ITERS)),
        in_specs=[
            pl.BlockSpec(memory_space=pltpu.SMEM),
            pl.BlockSpec(memory_space=pltpu.VMEM),
            pl.BlockSpec(memory_space=pl.ANY),
        ],
        out_specs=pl.BlockSpec(memory_space=pltpu.VMEM),
        out_shape=jax.ShapeDtypeStruct((32, n), F32),
        scratch_shapes=[pltpu.VMEM((half, n), F32)] + [part] * 6 + [full] * 2
        + [pltpu.VMEM((128, n), F32), pltpu.SemaphoreType.DMA],
        compiler_params=pltpu.CompilerParams(vmem_limit_bytes=40 * MIB),
        name="polar",
    )(place, own, oth)


AXES = ("gx", "gy")
CORES, SIDE, DEPTH = 2, 4, 8


def place_of(y, x, c, z):
    return ((y * SIDE + x) * CORES + c) * DEPTH + z


def ring_pairs(n, odd):
    pairs = [((i + odd) % n, (i + 1 + odd) % n) for i in range(0, n, 2)]
    return [p if k % 2 == 0 else p[::-1] for k, p in enumerate(pairs)]


def cube_groups():
    return [
        [place_of(y, x, c, z) for y in py for x in px for z in pz]
        for c in range(CORES)
        for py in ring_pairs(SIDE, c)
        for px in ring_pairs(SIDE, c)
        for pz in ring_pairs(DEPTH, c)
    ]


def swap(fn):
    return [
        (place_of(y, x, c, z), place_of(*fn(y, x, c, z)))
        for y in range(SIDE) for x in range(SIDE) for c in range(CORES) for z in range(DEPTH)
    ]


def mate(n, odd):
    table = {}
    for i in range(0, n, 2):
        a, b = (i + odd) % n, (i + 1 + odd) % n
        table[a], table[b] = b, a
    return table


def far(c):
    table = {}
    for a, b in ((0, 3), (4, 7), (2, 5), (6, 1)):
        a, b = (a + c) % DEPTH, (b + c) % DEPTH
        table[a], table[b] = b, a
    return table


SWAP_CORE = swap(lambda y, x, c, z: (y, x, 1 - c, z))
SWAP_Z = swap(lambda y, x, c, z: (y, x, c, mate(DEPTH, 1 - c)[z]))
SWAP_FAR = swap(lambda y, x, c, z: (y, x, c, far(c)[z]))

SWAP_X = swap(lambda y, x, c, z: (y, mate(SIDE, 1 - c)[x], c, z))
SWAP_Y = swap(lambda y, x, c, z: (mate(SIDE, 1 - c)[y], x, c, z))
SWAP_XY = swap(lambda y, x, c, z: (mate(SIDE, 1 - c)[y], mate(SIDE, 1 - c)[x], c, z))

SWAP_BOTH = swap(lambda y, x, c, z: (y, x, c, far(c)[mate(DEPTH, 1 - c)[z]]))


def send(value, pairs):
    return lax.ppermute(value, AXES, pairs)


def reduce_half(value, bit, pairs):
    half = value.shape[0] // 2
    away = lax.dynamic_slice_in_dim(value, (1 - bit) * half, half, 0)
    keep = lax.dynamic_slice_in_dim(value, bit * half, half, 0)
    return keep + send(away, pairs)


def gather_half(value, bit, pairs):
    other = send(value, pairs)
    return jnp.where(bit == 0, jnp.concatenate([value, other]), jnp.concatenate([other, value]))


def body(corpus, rotation, code_table, codebooks):
    rows, d = corpus.shape
    gx = lax.axis_index("gx")
    core = gx % CORES
    mine = (gx // CORES // SIDE % 2 * 2 + gx // CORES % 2).reshape(1)
    codes_t = code_table.T
    books_t = codebooks.transpose(0, 2, 1)
    held = [pltpu.with_memory_space_constraint(v, pltpu.HBM) for v in (codes_t, books_t, corpus, rotation)]
    scale = 1.0 / math.sqrt(rows * lax.axis_size("gx") * lax.axis_size("gy"))

    far_half, near_half = (1 - core).reshape(1), core.reshape(1)
    far_term, far_words = cross_half(far_half, mine, held[0], held[1], held[2], scale)
    arrived = send(far_term, SWAP_CORE)
    near_term, near_words = cross_second(near_half, codes_t, books_t, corpus, scale)

    groups = cube_groups()
    members = len(groups[0])
    summed = (near_term + arrived).reshape(members, -1, d)
    pieces = lax.all_to_all(summed, AXES, 0, 0, axis_index_groups=groups)
    part, *away = pick(mine, pieces)
    got = [send(v, p) for v, p in zip(away[::-1], (SWAP_XY, SWAP_Y, SWAP_X))]
    part = part + got[0] + got[1] + got[2]
    part, far_words = lax.optimization_barrier((part, far_words))
    others = [send(part, pairs) for pairs in (SWAP_BOTH, SWAP_FAR, SWAP_Z)]
    gaps = distortion(far_half, jnp.zeros((1, rows), F32), held[3], held[2], far_words)
    others, gaps = lax.optimization_barrier((others, gaps))
    part = part + others[0] + others[1] + others[2]
    got = [send(part, p) for p in (SWAP_XY, SWAP_Y, SWAP_X)]
    gathered = spread(mine, [part] + got[::-1], members)
    own = lax.all_to_all(gathered, AXES, 0, 0, axis_index_groups=groups)
    own = own.reshape(-1, d)
    own, near_words = lax.optimization_barrier((own, near_words))
    other = send(own, SWAP_CORE)
    gaps = distortion(near_half, gaps, held[3], held[2], near_words)
    other, gaps = lax.optimization_barrier((other, gaps))
    place = jnp.stack([core, gx // 4, gx % 4])
    return polar(place, own, other), gaps.reshape(rows)


def solution(mesh):
    return jax.shard_map(
        body,
        mesh=mesh,
        in_specs=(P(("gx", "gy"), None), P(), P(("gx", "gy"), None), P()),
        out_specs=(P("gx", None), P(("gx", "gy"))),
        check_vma=False,
    )
```

```python
import math, functools
import numpy as np
import jax, jax.numpy as jnp
from jax import lax
from jax.sharding import PartitionSpec as P
from jax.experimental import pallas as pl
from jax.experimental.pallas import tpu as pltpu

BF, F32 = jnp.bfloat16, jnp.float32
MIB = 1 << 20
BLK = 256
COARSE = 5
ITERS = 4
CHUNK = 16

def split(x):
    hi = x.astype(BF)
    return hi, (x - hi.astype(F32)).astype(BF)

def nt(a, b):
    return lax.dot_general(a, b, (((1,), (1,)), ((), ())), preferred_element_type=F32)

def nn(a, b):
    return lax.dot_general(a, b, (((1,), (0,)), ((), ())), preferred_element_type=F32)

def rebuild(codes, books, words, block):
    width = books.shape[1]
    word = lax.broadcasted_iota(jnp.int16, (books.shape[2], codes.shape[1]), 0)
    one, zero = jnp.ones((), BF), jnp.zeros((), BF)
    picks = codes[block * CHUNK:(block + 1) * CHUNK, :].astype(jnp.int16)
    for k in range(CHUNK):
        s = block * CHUNK + k
        hot = jnp.where(word == picks[k:k + 1, :], one, zero)
        words[s * width:(s + 1) * width, :] = nn(books[s], hot).astype(BF)


def first_kernel(scale, half_ref, mine_ref, codes_hbm, books_hbm, corpus_hbm, out, words_hbm, corpus, codes, books, words, sems):
    subs = books.shape[0]
    first = pl.multiple_of(half_ref[0] * subs, subs)
    tables = []
    for block in range(subs // CHUNK):
        at, to = pl.ds(first + block * CHUNK, CHUNK), pl.ds(block * CHUNK, CHUNK)
        tables.append(pltpu.make_async_copy(codes_hbm.at[at], codes.at[to], sems.at[2 * block]))
        tables.append(pltpu.make_async_copy(books_hbm.at[at], books.at[to], sems.at[2 * block + 1]))
    whole = pltpu.make_async_copy(corpus_hbm, corpus, sems.at[len(tables)])
    for load in tables + [whole]:
        load.start()
    for block in range(subs // CHUNK):
        tables[2 * block].wait()
        tables[2 * block + 1].wait()
        rebuild(codes, books, words, block)
    store = pltpu.make_async_copy(words, words_hbm, sems.at[len(tables) + 1])
    store.start()
    whole.wait()
    for k in range(corpus.shape[1] // BLK):
        c = slice(k * BLK, (k + 1) * BLK)
        out[:, c] = nn(words[...], corpus[:, c]) * scale
    store.wait()


def cross_half(half, mine, codes_t, books_t, corpus, scale):
    subs, width, size = books_t.shape
    rows, d = corpus.shape
    part = subs // 2
    return pl.pallas_call(
        functools.partial(first_kernel, scale),
        in_specs=[pl.BlockSpec(memory_space=pltpu.SMEM)] * 2 + [pl.BlockSpec(memory_space=pl.ANY)] * 3,
        out_specs=[pl.BlockSpec(memory_space=pltpu.VMEM), pl.BlockSpec(memory_space=pltpu.HBM), pl.BlockSpec(memory_space=pltpu.VMEM)],
        out_shape=[jax.ShapeDtypeStruct((part * width, d), F32), pltpu.HBM((part * width, rows), BF), jax.ShapeDtypeStruct((rows, d), BF)],
        scratch_shapes=[
            pltpu.VMEM((part, rows), jnp.int32),
            pltpu.VMEM((part, width, size), BF),
            pltpu.VMEM((part * width, rows), BF),
            pltpu.SemaphoreType.DMA((2 + 2 * (part // CHUNK),)),
        ],
        compiler_params=pltpu.CompilerParams(vmem_limit_bytes=24 * MIB),
        name="cross_half",
    )(half, mine, codes_t, books_t, corpus)


def second_kernel(scale, half_ref, codes_ref, books_ref, corpus_ref, out_ref, words_hbm, words, sem):
    subs = books_ref.shape[0] // 2
    first = pl.multiple_of(half_ref[0] * subs, subs)
    at = pl.ds(first, subs)
    for block in range(subs // CHUNK):
        rebuild(codes_ref.at[at], books_ref.at[at], words, block)
    store = pltpu.make_async_copy(words, words_hbm, sem)
    store.start()
    for k in range(corpus_ref.shape[1] // BLK):
        c = slice(k * BLK, (k + 1) * BLK)
        out_ref[:, c] = nn(words[...], corpus_ref[:, c]) * scale
    store.wait()


def cross_second(half, codes_t, books_t, corpus, scale):
    subs, width, _ = books_t.shape
    rows, d = corpus.shape
    part = subs // 2
    return pl.pallas_call(
        functools.partial(second_kernel, scale),
        in_specs=[pl.BlockSpec(memory_space=pltpu.SMEM)] + [pl.BlockSpec(memory_space=pltpu.VMEM)] * 3,
        out_specs=[pl.BlockSpec(memory_space=pltpu.VMEM), pl.BlockSpec(memory_space=pltpu.HBM)],
        out_shape=[jax.ShapeDtypeStruct((part * width, d), F32), pltpu.HBM((part * width, rows), BF)],
        scratch_shapes=[pltpu.VMEM((part * width, rows), BF), pltpu.SemaphoreType.DMA],
        compiler_params=pltpu.CompilerParams(vmem_limit_bytes=16 * MIB),
        name="cross_second",
    )(half, codes_t, books_t, corpus)


def pick_kernel(mine_ref, pieces_ref, *out_refs):
    rows = out_refs[0].shape[0]
    for k, out_ref in enumerate(out_refs):
        at = pl.ds(pl.multiple_of((mine_ref[0] ^ k) * rows, rows), rows)
        total = pieces_ref[0, at, :]
        for p in range(1, pieces_ref.shape[0]):
            total = total + pieces_ref[p, at, :]
        out_ref[...] = total


def pick(mine, pieces):
    _, rows, d = pieces.shape
    return pl.pallas_call(
        pick_kernel,
        in_specs=[pl.BlockSpec(memory_space=pltpu.SMEM), pl.BlockSpec(memory_space=pltpu.VMEM)],
        out_specs=[pl.BlockSpec(memory_space=pltpu.VMEM)] * 4,
        out_shape=[jax.ShapeDtypeStruct((rows // 4, d), F32)] * 4,
        compiler_params=pltpu.CompilerParams(vmem_limit_bytes=8 * MIB),
        name="pick",
    )(mine, pieces)


def spread_kernel(mine_ref, *refs):
    *part_refs, out_ref = refs
    rows = part_refs[0].shape[0]
    for k, part_ref in enumerate(part_refs):
        at = pl.ds(pl.multiple_of((mine_ref[0] ^ k) * rows, rows), rows)
        for p in range(out_ref.shape[0]):
            out_ref[p, at, :] = part_ref[...]


def spread(mine, parts, members):
    rows, d = parts[0].shape
    return pl.pallas_call(
        spread_kernel,
        in_specs=[pl.BlockSpec(memory_space=pltpu.SMEM)] + [pl.BlockSpec(memory_space=pltpu.VMEM)] * 4,
        out_specs=pl.BlockSpec(memory_space=pltpu.VMEM),
        out_shape=jax.ShapeDtypeStruct((members, 4 * rows, d), F32),
        compiler_params=pltpu.CompilerParams(vmem_limit_bytes=8 * MIB),
        name="spread",
    )(mine, *parts)


def dist_kernel(half_ref, sums_ref, corpus_ref, rot_hbm, words_hbm, out_ref, rot, words, sems):
    cols = words.shape[0]
    first = pl.multiple_of(half_ref[0] * cols, cols)
    loads = [
        pltpu.make_async_copy(rot_hbm.at[:, pl.ds(first, cols)], rot, sems.at[0]),
        pltpu.make_async_copy(words_hbm, words, sems.at[1]),
    ]
    for load in loads:
        load.start()
    for load in loads:
        load.wait()
    rotated = lax.dot_general(rot[...], corpus_ref[...], (((0,), (1,)), ((), ())), preferred_element_type=F32)
    gap = rotated - words[...].astype(F32)
    out_ref[...] = sums_ref[...] + jnp.sum(gap * gap, axis=0, keepdims=True)


def distortion(half, sums, rotation, corpus, words):
    rows, d = corpus.shape
    cols = words.shape[0]
    return pl.pallas_call(
        dist_kernel,
        in_specs=[pl.BlockSpec(memory_space=pltpu.SMEM), pl.BlockSpec(memory_space=pltpu.VMEM), pl.BlockSpec(memory_space=pltpu.VMEM)] + [pl.BlockSpec(memory_space=pl.ANY)] * 2,
        out_specs=pl.BlockSpec(memory_space=pltpu.VMEM),
        out_shape=jax.ShapeDtypeStruct((1, rows), F32),
        scratch_shapes=[
            pltpu.VMEM((d, cols), BF),
            pltpu.VMEM((cols, rows), BF),
            pltpu.SemaphoreType.DMA((2,)),
        ],
        compiler_params=pltpu.CompilerParams(vmem_limit_bytes=24 * MIB),
        name="distortion",
    )(half, sums, corpus, rotation, words)


def polar_polynomial(steps):
    poly = np.polynomial.polynomial
    e, out = np.array([0.0, 1.0]), np.array([1.0])
    for _ in range(steps):
        out = poly.polymul(out, poly.polyadd([1.0], 0.5 * e))
        sq = poly.polymul(e, e)
        e = poly.polyadd(0.75 * sq, 0.25 * poly.polymul(sq, e))
    return [float(v) for v in out]


def put(hi, lo, i, first, val):
    r = slice(i * BLK, (i + 1) * BLK)
    last = first + val.shape[1]
    hi[r, first:last], lo[r, first:last] = split(val)
    begin = max(first, (i + 1) * BLK)
    if begin < last:
        hi[begin:last, r], lo[begin:last, r] = split(val[:, begin - first:].T)


def inner(hi, lo, i, first, last, mul):
    r, c = slice(i * BLK, (i + 1) * BLK), slice(first, last)

    def times(a, b, at):
        return mul(a[r, :], b[at, :] if mul is nt else b[:, at])

    mixed = times(hi, lo, c)
    if first > i * BLK:
        mixed = mixed + times(lo, hi, c)
    else:
        corner = mixed[:, :BLK] + mixed[:, :BLK].T
        if last > first + BLK:
            rest = mixed[:, BLK:] + times(lo, hi, slice(first + BLK, last))
            mixed = jnp.concatenate([corner, rest], axis=1)
        else:
            mixed = corner
    return times(hi, hi, c) + mixed


def thin(u, hi, lo):
    h, l = split(u)
    m = u.shape[0]
    p = nn(jnp.concatenate([h, l], axis=0), hi[...])
    return p[:m] + (p[m:] + nn(h, lo[...]))


def polar_kernel(coef, place_ref, own_ref, oth_hbm, out_ref, oth, yh, yl, gh, gl, bh, bl, gf, bf, turned, sem):
    n = yh.shape[0]
    half = n // 2
    blocks = n // BLK
    rows = out_ref.shape[0]
    load = pltpu.make_async_copy(oth_hbm, oth, sem)
    load.start()
    col = pl.multiple_of(place_ref[1] * 128, 128)
    yh[:half, :], yl[:half, :] = split(own_ref[...])
    turned[:, :half] = own_ref[:, pl.ds(col, 128)].T
    total = jnp.zeros((), F32)
    for i in range(half // BLK):
        g = inner(yh, yl, i, i * BLK, half, nt)
        gf[i * BLK:(i + 1) * BLK, i * BLK:half] = g
        put(gh, gl, i, i * BLK, g)
        sq = g * g
        total = total + 2.0 * jnp.sum(sq) - jnp.sum(sq[:, :BLK])
    load.wait()
    yh[half:, :], yl[half:, :] = split(oth[...])
    turned[:, half:] = oth[:, pl.ds(col, 128)].T
    for i in range(blocks):
        first = max(half, i * BLK)
        g = inner(yh, yl, i, first, n, nt)
        gf[i * BLK:(i + 1) * BLK, first:] = g
        put(gh, gl, i, first, g)
        sq = g * g
        total = total + 2.0 * jnp.sum(sq)
        if i * BLK >= half:
            total = total - jnp.sum(sq[:, :BLK])
    root = lax.rsqrt(jnp.full((8, 128), total + 1e-06, F32))
    f2 = jnp.max(root)
    f1 = jnp.max(jnp.sqrt(root))
    for i in range(blocks):
        at = slice(i * BLK, (i + 1) * BLK), slice(i * BLK, n)
        b = (2.0 * f2) * gf[at] - (f2 * f2) * inner(gh, gl, i, i * BLK, n, nn)
        bf[at] = b
        put(bh, bl, i, i * BLK, b)
    for i in range(blocks):
        at = slice(i * BLK, (i + 1) * BLK), slice(i * BLK, n)
        put(yh, yl, i, i * BLK, 2.0 * bf[at] - inner(bh, bl, i, i * BLK, n, nn))

    first = turned[pl.ds(pl.multiple_of(place_ref[2] * rows, rows), rows), :] * f1
    pair = jnp.concatenate([first, first - f2 * thin(first, gh, gl)], axis=0)
    quad = jnp.concatenate([pair, pair - thin(pair, bh, bl)], axis=0)

    def mix(k):
        terms = [coef[4 * k + q] * quad[q * rows:(q + 1) * rows] for q in range(4) if 4 * k + q < len(coef)]
        return functools.reduce(lambda a, b: a + b, terms)

    u = mix((len(coef) - 1) // 4)
    for k in range((len(coef) - 1) // 4 - 1, -1, -1):
        step = nn(u.astype(BF), yh[...]) if k >= COARSE else thin(u, yh, yl)
        u = u - step + mix(k)
    u = u * math.sqrt(n)
    low = place_ref[0] == 0
    out_ref[:, :half] = jnp.where(low, u[:, :half], u[:, half:])
    out_ref[:, half:] = jnp.where(low, u[:, half:], u[:, :half])


def polar(place, own, oth):
    half, n = own.shape
    part, full = pltpu.VMEM((n, n), BF), pltpu.VMEM((n, n), F32)
    return pl.pallas_call(
        functools.partial(polar_kernel, polar_polynomial(ITERS)),
        in_specs=[
            pl.BlockSpec(memory_space=pltpu.SMEM),
            pl.BlockSpec(memory_space=pltpu.VMEM),
            pl.BlockSpec(memory_space=pl.ANY),
        ],
        out_specs=pl.BlockSpec(memory_space=pltpu.VMEM),
        out_shape=jax.ShapeDtypeStruct((32, n), F32),
        scratch_shapes=[pltpu.VMEM((half, n), F32)] + [part] * 6 + [full] * 2
        + [pltpu.VMEM((128, n), F32), pltpu.SemaphoreType.DMA],
        compiler_params=pltpu.CompilerParams(vmem_limit_bytes=40 * MIB),
        name="polar",
    )(place, own, oth)


AXES = ("gx", "gy")
CORES, SIDE, DEPTH = 2, 4, 8


def place_of(y, x, c, z):
    return ((y * SIDE + x) * CORES + c) * DEPTH + z


def ring_pairs(n, odd):
    pairs = [((i + odd) % n, (i + 1 + odd) % n) for i in range(0, n, 2)]
    return [p if k % 2 == 0 else p[::-1] for k, p in enumerate(pairs)]


def cube_groups():
    return [
        [place_of(y, x, c, z) for y in py for x in px for z in pz]
        for c in range(CORES)
        for py in ring_pairs(SIDE, c)
        for px in ring_pairs(SIDE, c)
        for pz in ring_pairs(DEPTH, c)
    ]


def swap(fn):
    return [
        (place_of(y, x, c, z), place_of(*fn(y, x, c, z)))
        for y in range(SIDE) for x in range(SIDE) for c in range(CORES) for z in range(DEPTH)
    ]


def mate(n, odd):
    table = {}
    for i in range(0, n, 2):
        a, b = (i + odd) % n, (i + 1 + odd) % n
        table[a], table[b] = b, a
    return table


def far(c):
    table = {}
    for a, b in ((0, 3), (4, 7), (2, 5), (6, 1)):
        a, b = (a + c) % DEPTH, (b + c) % DEPTH
        table[a], table[b] = b, a
    return table


SWAP_CORE = swap(lambda y, x, c, z: (y, x, 1 - c, z))
SWAP_Z = swap(lambda y, x, c, z: (y, x, c, mate(DEPTH, 1 - c)[z]))
SWAP_FAR = swap(lambda y, x, c, z: (y, x, c, far(c)[z]))

SWAP_X = swap(lambda y, x, c, z: (y, mate(SIDE, 1 - c)[x], c, z))
SWAP_Y = swap(lambda y, x, c, z: (mate(SIDE, 1 - c)[y], x, c, z))
SWAP_XY = swap(lambda y, x, c, z: (mate(SIDE, 1 - c)[y], mate(SIDE, 1 - c)[x], c, z))

SWAP_BOTH = swap(lambda y, x, c, z: (y, x, c, far(c)[mate(DEPTH, 1 - c)[z]]))


def send(value, pairs):
    return lax.ppermute(value, AXES, pairs)


def reduce_half(value, bit, pairs):
    half = value.shape[0] // 2
    away = lax.dynamic_slice_in_dim(value, (1 - bit) * half, half, 0)
    keep = lax.dynamic_slice_in_dim(value, bit * half, half, 0)
    return keep + send(away, pairs)


def gather_half(value, bit, pairs):
    other = send(value, pairs)
    return jnp.where(bit == 0, jnp.concatenate([value, other]), jnp.concatenate([other, value]))


def body(corpus, rotation, code_table, codebooks):
    rows, d = corpus.shape
    gx = lax.axis_index("gx")
    core = gx % CORES
    mine = (gx // CORES // SIDE % 2 * 2 + gx // CORES % 2).reshape(1)
    codes_t = code_table.T
    books_t = codebooks.transpose(0, 2, 1)
    held = [pltpu.with_memory_space_constraint(v, pltpu.HBM) for v in (codes_t, books_t, corpus, rotation)]
    scale = 1.0 / math.sqrt(rows * lax.axis_size("gx") * lax.axis_size("gy"))

    far_half, near_half = (1 - core).reshape(1), core.reshape(1)
    far_term, far_words, near_corpus = cross_half(far_half, mine, held[0], held[1], held[2], scale)
    arrived = send(far_term, SWAP_CORE)
    near_term, near_words = cross_second(near_half, codes_t, books_t, near_corpus, scale)

    groups = cube_groups()
    members = len(groups[0])
    summed = (near_term + arrived).reshape(members, -1, d)
    pieces = lax.all_to_all(summed, AXES, 0, 0, axis_index_groups=groups)
    part, *away = pick(mine, pieces)
    got = [send(v, p) for v, p in zip(away[::-1], (SWAP_XY, SWAP_Y, SWAP_X))]
    part = part + got[0] + got[1] + got[2]
    part, far_words = lax.optimization_barrier((part, far_words))
    others = [send(part, pairs) for pairs in (SWAP_BOTH, SWAP_FAR, SWAP_Z)]
    gaps = distortion(far_half, jnp.zeros((1, rows), F32), held[3], near_corpus, far_words)
    others, gaps = lax.optimization_barrier((others, gaps))
    part = part + others[0] + others[1] + others[2]
    got = [send(part, p) for p in (SWAP_XY, SWAP_Y, SWAP_X)]
    gathered = spread(mine, [part] + got[::-1], members)
    own = lax.all_to_all(gathered, AXES, 0, 0, axis_index_groups=groups)
    own = own.reshape(-1, d)
    own, near_words = lax.optimization_barrier((own, near_words))
    other = send(own, SWAP_CORE)
    gaps = distortion(near_half, gaps, held[3], near_corpus, near_words)
    other, gaps = lax.optimization_barrier((other, gaps))
    place = jnp.stack([core, gx // 4, gx % 4])
    return polar(place, own, other), gaps.reshape(rows)


def solution(mesh):
    return jax.shard_map(
        body,
        mesh=mesh,
        in_specs=(P(("gx", "gy"), None), P(), P(("gx", "gy"), None), P()),
        out_specs=(P("gx", None), P(("gx", "gy"))),
        check_vma=False,
    )
```
